128 devices in a mesh: attn: 4 (over y), expert: 32 (over z, x, core).
Axes of the slice: x: 4, y: 4, z: 4, core: 2. Of those that a mesh axis runs over, the one named last changes fastest.
Arguments:
- residual: float32 [512, 4096], P('attn', 'expert'), may hold values from -63 to 63
- queries: bfloat16 [512, 8192], P('expert', 'attn'), may hold values from -12 to 12
- keys: bfloat16 [512, 1024, 512], P('expert', None, 'attn'), may hold values from -6 to 6
- values: bfloat16 [512, 1024, 512], P('expert', None, 'attn'), may hold values from -6 to 6
- lengths: int32 [512], P('expert'), may hold values from 1 to 1024, 262144 in all
- out_weight: bfloat16 [8192, 4096], P('attn', 'expert'), may hold values from -0.0625 to 0.0625
- norm_gain: float32 [4096], P('expert'), may hold values from 0.1 to 1.9
- expert_ids: int32 [512, 8], P('attn'), may hold values from 0 to 127, all different within a row; in each aligned block of 128 rows (0 to 127, 128 to 255, ...) at most 16 rows name the same one
- gates: float32 [512, 8], P('attn'), may hold values from 0.05 to 0.5
- gate_up: bfloat16 [128, 4096, 1536], P(('attn', 'expert')), may hold values from -0.09375 to 0.09375
- down: bfloat16 [128, 768, 4096], P(('attn', 'expert')), may hold values from -0.21875 to 0.21875
Outputs:
- layer_out: float32 [512, 4096], P('attn', 'expert')
The draws below stay inside these ranges and needn't reach their ends.
Inputs may be any that keep to these rules, and one draw needn't show every extreme that they name: `expert_ids`: among the 128 tokens of each index of attn (aligned blocks of rows), no expert is named more than 16 times; a token's 8 experts differ.
All inputs are finite; a program needn't handle non-finite values. No bound on the sum of `lengths` on one device may be relied on, other than what follows from the above.
Results may differ from the reference program's by a relative error of at most 0.0015.
Values may be sent and summed in bfloat16 or wider, within the bound.
A program may use at most 128 MiB of HBM per device.

```python
import math
import jax
import jax.numpy as jnp
import numpy as np
from jax import lax

D = 4096
QH = 64
KVH = 4
HD = 128
EH = 768
TOPK = 8
LEN = 1024
TOKENS = 512
TOK_ROW = 128
EXPERTS = 128
CAP = 16
N_ATTN = 4


def draw_queries(key, part):
    key = jax.random.fold_in(key, 21)
    field = jnp.clip(jax.random.normal(key, (TOKENS, QH * HD), jnp.float32), -6.0, 6.0)
    return field.astype(jnp.bfloat16)


def draw_keys(key, part):
    key = jax.random.fold_in(key, 22)
    shape = (TOKENS, LEN, KVH * HD)
    field = jnp.clip(jax.random.normal(key, shape, jnp.float32), -6.0, 6.0)
    return field.astype(jnp.bfloat16)


def draw_residual(key, part):
    key = jax.random.fold_in(key, 23)
    key_rows, key_cols, key_body = jax.random.split(key, 3)
    row_scale = jnp.exp(jax.random.uniform(key_rows, (TOKENS, 1), jnp.float32, math.log(0.3), math.log(3.0)))
    col_scale = jnp.exp(jax.random.uniform(key_cols, (1, D), jnp.float32, math.log(0.3), math.log(3.0)))
    place = (jnp.arange(D).astype(jnp.float32) / max(D - 1, 1))[None, :]
    ramp = jnp.sqrt(1.0 + 2.0 * place)
    field = jnp.clip(jax.random.normal(key_body, (TOKENS, D), jnp.float32), -4.0, 4.0)
    return (field * row_scale * col_scale * ramp).astype(jnp.float32)


def levels(own_key, shape, shards, smallest, largest):
    def one(dim, blocks):
        draws = jax.random.uniform(jax.random.fold_in(jax.random.fold_in(own_key, 6), dim), (blocks,), jnp.float32, smallest / len(shards), largest / len(shards))
        return jnp.repeat(jnp.exp(draws), shape[dim] // blocks).reshape((-1,) + (1,) * (len(shape) - dim - 1))

    factor_of = one(*shards[0])
    for cut in shards[1:]:
        factor_of = factor_of * one(*cut)
    return factor_of


def split_up(amount, total, limit, lean):
    portions = [(1 << 20) // math.isqrt(rank ** lean) + 1 for rank in range(2, amount + 1)]
    surplus, holding = total - limit - (amount - 1), [1] * (amount - 1)
    while surplus > 0:
        candidates = [i for i in range(amount - 1) if holding[i] < limit]
        whole, remaining = sum([portions[i] for i in candidates]), surplus
        for i in candidates:
            extra = min(limit - holding[i], max(1, remaining * portions[i] // whole), surplus)
            holding[i] = holding[i] + extra
            surplus = surplus - extra
    return np.array([limit] + holding)


def ragged_sizes(rng, count, total, reach, lean):
    if count == 2:
        one = jax.random.randint(rng, (), max(1, total - reach), min(reach, total - 1) + 1)
        return jnp.stack([one, total - one])
    tallies = jnp.asarray(split_up(count, total, reach, lean), jnp.int32)
    pairs = (count - 1) // 2
    donor, taker = tallies[1:1 + 2 * pairs:2], tallies[2:2 + 2 * pairs:2]
    slack = jnp.minimum(donor - 1, reach - taker)
    passed = jax.random.randint(jax.random.fold_in(rng, 1), (pairs,), 0, 1 << 20) % (slack + 1)
    tallies = tallies.at[1:1 + 2 * pairs:2].set(donor - passed).at[2:2 + 2 * pairs:2].set(taker + passed)
    return tallies[jax.random.permutation(jax.random.fold_in(rng, 2), count)]


def deal_out(rng, own, number, rows, amount, top, limit, slope):
    order = jax.random.permutation(rng, amount)
    crowded, common = load_shares(amount, rows * top, limit, slope, True), load_shares(amount, rows * top, limit, slope, False)
    places = jnp.arange(amount)

    def named(sizes, rotation):
        used = int((sizes > 0).sum())
        fixed = max(1, used // 4)
        passed = fixed + (places - fixed + rotation * (used - fixed)) % max(1, amount - fixed)
        return jnp.zeros((amount,), jnp.int32).at[order[jnp.where(places < fixed, places, passed)]].set(jnp.asarray(sizes, jnp.int32))

    sizes = jnp.where(number % 4 == 0, named(crowded, number // 4), named(common, number - number // 4 - 1))
    mixed = jax.random.permutation(jax.random.fold_in(own, 3), amount)
    giver, sink = mixed[0:amount // 2 * 2:2], mixed[1:amount // 2 * 2:2]
    margin = jnp.minimum(sizes[giver] - 1, limit - sizes[sink]) // 2
    margin = jnp.where((giver == order[0]) | (sink == order[0]) | (sizes[sink] == 0), 0, jnp.maximum(margin, 0))
    passed = jax.random.randint(jax.random.fold_in(own, 4), (amount // 2,), 0, 1 << 20) % (margin + 1)
    sizes = sizes.at[giver].add(-passed).at[sink].add(passed)
    labels = jnp.searchsorted(jnp.cumsum(sizes), jnp.arange(rows * top), side="right").astype(jnp.int32)
    table = labels.reshape(top, rows).T
    table = table[jax.random.permutation(jax.random.fold_in(own, 1), rows)]
    rotation = jax.random.randint(jax.random.fold_in(own, 2), (rows, 1), 0, top)
    return jnp.take_along_axis(table, (jnp.arange(top)[None, :] + rotation) % top, axis=1)


def load_shares(count, total, reach, lean, full):
    weights = [(1 << 20) // math.isqrt(standing ** lean) + 1 for standing in range(1, count + 1)]
    largest = reach if full else min(reach, max(-(-total // count), total * weights[0] // sum(weights)))
    least = 1 if total - largest >= count - 1 else 0
    holding, surplus = [largest] + [least] * (count - 1), total - largest - least * (count - 1)
    while surplus > 0:
        candidates = [i for i in range(1, count) if holding[i] < largest] or [i for i in range(1, count) if holding[i] < reach]
        whole, remaining = sum([weights[i] for i in candidates]), surplus
        for i in candidates:
            addition = min(reach - holding[i], max(1, remaining * weights[i] // whole), surplus)
            holding[i] = holding[i] + addition
            surplus = surplus - addition
    return np.array(holding)


def normal_values(rng, extent, scale, reach, shards=(), kind=jnp.bfloat16):
    gain = levels(rng, extent, shards, -0.22, 0.18) if shards else 1.0
    drawn = jax.random.normal(rng, extent, jnp.float32) * scale * gain
    return jnp.minimum(jnp.maximum(drawn, -reach), reach).astype(kind)


def setup_inputs(seed: int = 0) -> dict:
    arg_keys = jax.random.split(jax.random.key(seed), 12)
    residual = draw_residual(jax.random.fold_in(arg_keys[11], 71), 0)
    queries = draw_queries(jax.random.fold_in(arg_keys[11], 71), 0)
    keys = draw_keys(jax.random.fold_in(arg_keys[11], 71), 0)
    values = normal_values(arg_keys[3], (TOKENS, LEN, KVH * HD), 1.0, 6.0, ((0, 32), (2, 4)))
    lengths = ragged_sizes(arg_keys[4], TOKENS, TOKENS * LEN // 2, LEN, 2).astype(jnp.int32)
    out_weight = normal_values(arg_keys[5], (QH * HD, D), (QH * HD) ** -0.5, 0.0625, ((0, 4), (1, 32)))
    norm_gain = jnp.clip(1.0 + 0.18 * jax.random.normal(arg_keys[6], (D,), jnp.float32), 0.1, 1.9)
    expert_ids_keys = jax.random.split(jax.random.fold_in(arg_keys[7], 1), TOKENS // TOK_ROW)
    expert_ids_turns = jax.random.permutation(jax.random.fold_in(arg_keys[7], 3), TOKENS // TOK_ROW)
    expert_ids = jax.vmap(lambda own, number: deal_out(jax.random.fold_in(arg_keys[7], 2), own, number, TOK_ROW, EXPERTS, TOPK, CAP, 2))(expert_ids_keys, expert_ids_turns).reshape((TOKENS, TOPK))
    gates = jnp.clip(jnp.exp(math.log(0.5) - 2.3025851 * jax.random.uniform(arg_keys[8], (TOKENS, TOPK), jnp.float32) ** levels(arg_keys[8], (TOKENS, TOPK), ((0, 4),), -0.2, 0.2)), 0.05, 0.5)
    gate_up = normal_values(arg_keys[9], (EXPERTS, D, 2 * EH), D ** -0.5, 0.09375, ((0, 128),))
    down = normal_values(arg_keys[10], (EXPERTS, EH, D), EH ** -0.5, 0.21875, ((0, 128),))
    return {"residual": residual, "queries": queries, "keys": keys, "values": values, "lengths": lengths, "out_weight": out_weight, "norm_gain": norm_gain, "expert_ids": expert_ids, "gates": gates, "gate_up": gate_up, "down": down}


def expert_apply(rows_in, gate_up_k, down_k):
    mixed = jnp.dot(rows_in, gate_up_k, preferred_element_type=jnp.float32)
    width = down_k.shape[0]
    inner = (jax.nn.silu(mixed[:, :width]) * mixed[:, width:]).astype(jnp.bfloat16)
    return jnp.dot(inner, down_k, preferred_element_type=jnp.float32).astype(jnp.bfloat16)

def reference(residual, queries, keys, values, lengths, out_weight, norm_gain, expert_ids, gates, gate_up, down):
    group = QH // KVH
    query_all = queries.astype(jnp.float32).reshape(TOKENS, KVH, group, HD)
    key_all = keys.astype(jnp.float32).reshape(TOKENS, LEN, KVH, HD)
    value_all = values.astype(jnp.float32).reshape(TOKENS, LEN, KVH, HD)
    scores = jnp.einsum('thgd,tlhd->thgl', query_all, key_all) * (1.0 / math.sqrt(HD))
    valid = jnp.arange(LEN, dtype=jnp.int32)[None, None, None, :] < lengths.astype(jnp.int32)[:, None, None, None]
    scores = jnp.where(valid, scores, -1e+30)
    peak = lax.optimization_barrier(jnp.max(scores, axis=-1, keepdims=True))
    expo = jnp.where(valid, jnp.exp(scores - peak), 0.0)
    weights = (expo / lax.optimization_barrier(jnp.sum(expo, axis=-1, keepdims=True))).astype(jnp.bfloat16)
    attended = jnp.einsum('thgl,tlhd->thgd', weights.astype(jnp.float32), value_all)
    attended = attended.astype(jnp.bfloat16).reshape(TOKENS, QH * HD)
    hidden_state = residual.astype(jnp.float32) + jnp.dot(attended, out_weight, preferred_element_type=jnp.float32)
    square = lax.optimization_barrier(jnp.sum(hidden_state * hidden_state, axis=1, keepdims=True))
    normed = (hidden_state * lax.rsqrt(square / D + 1e-06) * norm_gain).astype(jnp.bfloat16)
    order = (TOKENS - jnp.arange(TOKENS, dtype=jnp.int32)).astype(jnp.int32)

    def step(total, packed):
        gate_up_k, down_k, index = packed
        routed = expert_ids == index
        weight = lax.optimization_barrier(jnp.sum(jnp.where(routed, gates, 0.0), axis=1))
        score = jnp.where(jnp.any(routed, axis=1), order, jnp.zeros_like(order))
        unused, picked = lax.top_k(score, N_ATTN * CAP)
        produced = expert_apply(normed[picked], gate_up_k, down_k)
        total = total.at[picked].add(weight[picked][:, None] * produced.astype(jnp.float32))
        return (total, None)
    start = jnp.zeros((TOKENS, D), jnp.float32)
    moe, unused = lax.scan(step, start, (gate_up, down, jnp.arange(EXPERTS, dtype=jnp.int32)))
    return hidden_state + moe
```

```python
import functools
import math

import jax
import jax.numpy as jnp
from jax import lax
from jax.experimental import pallas as pl
from jax.experimental.pallas import tpu as pltpu
from jax.sharding import PartitionSpec as P

HD = 128
CAP = 16
CORES = 2
PARTS = 3
F32 = jnp.float32
BF16 = jnp.bfloat16
MESH = pl.DeviceIdType.MESH
NT = (((1,), (1,)), ((), ()))


def dot(left, right):
    return jnp.dot(left, right, preferred_element_type=F32)


def dot_nt(left, right):
    return lax.dot_general(left, right, NT, preferred_element_type=F32)


def split3(value):
    high = value.astype(BF16)
    rest = value - high.astype(F32)
    middle = rest.astype(BF16)
    low = (rest - middle.astype(F32)).astype(BF16)
    return high, middle, low


def layer_kernel(
    cfg,
    lengths,
    residual,
    queries,
    keys,
    values,
    out_weight,
    gain,
    ids,
    gates,
    gate_up,
    down,
    out,
    q_in,
    q_rows,
    o_rows,
    k_buf,
    v_buf,
    w_buf,
    res_buf,
    gain_buf,
    ids_all,
    gates_all,
    att,
    part_send,
    part_recv,
    normed,
    select,
    comb_high,
    comb_low,
    x_send,
    x_recv,
    gate_up_buf,
    down_buf,
    mixed,
    y_send,
    y_recv,
    moe_send,
    moe_recv,
    in_sem,
    k_sem,
    v_sem,
    gate_sem,
    w_send,
    w_recv,
    ids_send,
    ids_recv,
    gates_send,
    gates_recv,
    att_send,
    att_recv,
    rs_send,
    rs_recv,
    norm_send,
    norm_recv,
    xs_sem,
    xr_sem,
    ys_sem,
    yr_sem,
    ms_sem,
    mr_sem,
):
    n_attn, n_z, n_x, req, heads, width = cfg
    n_exp = n_z * n_x * CORES
    chips = n_z * n_x
    per_z = n_x * CORES
    block = per_z * req
    half = n_x * req
    features = n_exp * HD
    slots = n_exp * CAP
    rows = n_attn * CAP
    a = lax.axis_index("attn")
    e = lax.axis_index("expert")
    core = lax.rem(e, CORES)
    chip = lax.div(e, CORES)
    x = lax.rem(chip, n_x)
    z = lax.div(chip, n_x)
    sibling = chip * CORES + (1 - core)

    def wrap(value, size):
        return lax.rem(value, size)

    barrier = pltpu.get_barrier_semaphore()

    def greet(d, carry):
        pl.semaphore_signal(
            barrier, inc=1, device_id=(a, wrap(e + d, n_exp)), device_id_type=MESH
        )
        return carry

    lax.fori_loop(1, n_exp, greet, 0)
    for i in range(1, n_attn):
        for other in range(CORES):
            pl.semaphore_signal(
                barrier,
                inc=1,
                device_id=(wrap(a + i, n_attn), chip * CORES + other),
                device_id_type=MESH,
            )

    group = k_buf.shape[0] // k_sem.shape[0]
    n_group = k_sem.shape[0]
    load_q = pltpu.make_async_copy(queries, q_in, in_sem.at[0])
    load_q.start()

    def load_k(g):
        span = pl.ds(g * group, group)
        return pltpu.make_async_copy(keys.at[span], k_buf.at[span], k_sem.at[g])

    def load_v(g):
        span = pl.ds(g * group, group)
        return pltpu.make_async_copy(values.at[span], v_buf.at[span], v_sem.at[g])

    for g in range(n_group):
        load_k(g).start()
        load_v(g).start()
    own_columns = pl.ds(pl.multiple_of(core * HD, HD), HD)
    load_w = pltpu.make_async_copy(out_weight, w_buf.at[:, own_columns], in_sem.at[1])
    load_res = pltpu.make_async_copy(residual, res_buf, in_sem.at[2])
    load_gain = pltpu.make_async_copy(gain, gain_buf, in_sem.at[3])
    load_ids = pltpu.make_async_copy(ids, ids_all.at[a], in_sem.at[4])
    load_gates = pltpu.make_async_copy(gates, gates_all.at[a], in_sem.at[5])
    for load in (load_w, load_res, load_gain, load_ids, load_gates):
        load.start()

    load_q.wait()
    pairs = (heads * req, heads * req)
    first = lax.broadcasted_iota(jnp.int32, pairs, 0)
    second = lax.broadcasted_iota(jnp.int32, pairs, 1)
    by_request = (lax.div(first, heads) == lax.rem(second, req)) & (
        lax.rem(first, heads) == lax.div(second, req)
    )
    stacked = jnp.concatenate([q_in[:, h * HD : (h + 1) * HD] for h in range(heads)], axis=0)
    q_rows[...] = dot(by_request.astype(F32).astype(BF16), stacked).astype(BF16)
    span = k_buf.shape[1]
    position = lax.broadcasted_iota(jnp.int32, (heads, span), 1)
    for g in range(n_group):
        load_k(g).wait()
        load_v(g).wait()
        for i in range(g * group, (g + 1) * group):
            query = q_rows[i * heads : (i + 1) * heads, :]
            scores = dot_nt(query, k_buf[i]) * (1.0 / math.sqrt(HD))
            scores = jnp.where(position < lengths[i], scores, -1e30)
            peak = jnp.max(scores, axis=1, keepdims=True)
            expo = jnp.exp(scores - peak)
            weights = (expo / jnp.sum(expo, axis=1, keepdims=True)).astype(BF16)
            o_rows[i * heads : (i + 1) * heads, :] = dot(weights, v_buf[i]).astype(BF16)
    by_head = (lax.div(first, req) == lax.rem(second, heads)) & (
        lax.rem(first, req) == lax.div(second, heads)
    )
    own = dot(by_head.astype(F32).astype(BF16), o_rows[...])
    att[z, x] = own.astype(BF16).reshape(heads, req, HD)

    pl.semaphore_wait(barrier, n_exp - 1 + CORES * (n_attn - 1))

    def push_att(d):
        to = wrap(chip + d, chips)
        return pltpu.make_async_remote_copy(
            src_ref=att.at[z, x],
            dst_ref=att.at[z, x],
            send_sem=att_send.at[d],
            recv_sem=att_recv.at[chip],
            device_id=(a, to * CORES + core),
            device_id_type=MESH,
        )

    def start_att(d, carry):
        push_att(d).start()
        return carry

    lax.fori_loop(1, chips, start_att, 0)

    push_w = pltpu.make_async_remote_copy(
        src_ref=out_weight,
        dst_ref=w_buf.at[:, own_columns],
        send_sem=w_send,
        recv_sem=w_recv,
        device_id=(a, sibling),
        device_id_type=MESH,
    )
    push_w.start()

    def push_ids(i):
        return pltpu.make_async_remote_copy(
            src_ref=ids,
            dst_ref=ids_all.at[a],
            send_sem=ids_send.at[i],
            recv_sem=ids_recv.at[a],
            device_id=(wrap(a + i, n_attn), e),
            device_id_type=MESH,
        )

    def push_gates(i):
        return pltpu.make_async_remote_copy(
            src_ref=gates,
            dst_ref=gates_all.at[a],
            send_sem=gates_send.at[i],
            recv_sem=gates_recv.at[a],
            device_id=(wrap(a + i, n_attn), e),
            device_id_type=MESH,
        )

    for i in range(1, n_attn):
        push_ids(i).start()
        push_gates(i).start()

    depth = per_z * HD

    def load_gate_up(g):
        part = pl.ds(pl.multiple_of(g * depth, depth), depth)
        return pltpu.make_async_copy(
            gate_up.at[0, part, :], gate_up_buf.at[part, :], gate_sem.at[g]
        )

    load_down = pltpu.make_async_copy(down.at[0], down_buf, in_sem.at[6])
    for g in range(n_z):
        load_gate_up(g).start()
    load_down.start()

    for load in (load_ids, load_gates):
        load.wait()
    earlier = (
        lax.broadcasted_iota(jnp.int32, (block, block), 0)
        < lax.broadcasted_iota(jnp.int32, (block, block), 1)
    ).astype(F32).astype(BF16)
    spread_row = lax.broadcasted_iota(jnp.int32, (slots, n_exp), 0)
    spread_col = lax.broadcasted_iota(jnp.int32, (slots, n_exp), 1)
    spread = (
        ((spread_row >= spread_col * CAP) & (spread_row < (spread_col + 1) * CAP))
        .astype(F32)
        .astype(BF16)
    )
    slot = lax.rem(lax.broadcasted_iota(jnp.int32, (slots, block), 0), CAP).astype(F32)
    named = lax.broadcasted_iota(jnp.int32, (n_exp, block), 0) + a * n_exp
    top = ids_all.shape[1]
    for i in range(n_attn):
        b = wrap(a + i, n_attn)
        if i > 0:
            pltpu.make_async_copy(ids, ids_all.at[b], ids_recv.at[b]).wait()
            pltpu.make_async_copy(gates, gates_all.at[b], gates_recv.at[b]).wait()
        ids_b = ids_all[b]
        gates_b = gates_all[b]
        chosen = jnp.zeros((n_exp, block), F32)
        weight = jnp.zeros((n_exp, block), F32)
        for k in range(top):
            hit = ids_b[k : k + 1, :] == named
            chosen = chosen + jnp.where(hit, 1.0, 0.0)
            weight = weight + jnp.where(hit, gates_b[k : k + 1, :], 0.0)
        rank = dot(chosen.astype(BF16), earlier)
        high = weight.astype(BF16)
        low = (weight - high.astype(F32)).astype(BF16)
        table = jnp.concatenate([rank.astype(BF16), chosen.astype(BF16), high, low], axis=1)
        wide = dot(spread, table)
        here = wide[:, :block] == slot
        select[b] = jnp.where(here, wide[:, block : 2 * block], 0.0).astype(BF16)
        comb_high[b] = jnp.where(here, wide[:, 2 * block : 3 * block], 0.0).T.astype(BF16)
        comb_low[b] = jnp.where(here, wide[:, 3 * block :], 0.0).T.astype(BF16)

    load_w.wait()
    push_w.wait_recv()

    def push_part(i, other):
        return pltpu.make_async_remote_copy(
            src_ref=part_send.at[i, other],
            dst_ref=part_recv.at[a, core],
            send_sem=rs_send.at[i * CORES + other],
            recv_sem=rs_recv.at[a * CORES + core],
            device_id=(wrap(a + i, n_attn), chip * CORES + other),
            device_id_type=MESH,
        )

    for i in [*range(1, n_attn), 0]:
        b = wrap(a + i, n_attn)
        for xx in range(n_x):
            @pl.when(jnp.logical_not((b == z) & (x == xx)))
            def _():
                pltpu.make_async_copy(
                    att.at[b, xx], att.at[b, xx], att_recv.at[b * n_x + xx]
                ).wait()

        left = jnp.concatenate(
            [att[b, :, h].reshape(half, HD) for h in range(heads)], axis=1
        )
        part = dot(left, w_buf[...])
        for other in range(CORES):
            part_send[i, other] = part[:, other * HD : (other + 1) * HD]
        if i > 0:
            for other in range(CORES):
                push_part(i, other).start()
        else:
            push_part(0, 1 - core).start()
            part_recv[a, core] = part_send[0, core]

    for i in range(n_attn):
        b = wrap(a + i, n_attn)
        for other in range(CORES):
            def arrived(b=b, other=other):
                pltpu.make_async_copy(
                    part_recv.at[b, other],
                    part_recv.at[b, other],
                    rs_recv.at[b * CORES + other],
                ).wait()

            if i > 0:
                arrived()
            else:
                pl.when(core != other)(arrived)

    load_res.wait()
    load_gain.wait()
    totals = []
    for other in range(CORES):
        total = part_recv[0, other]
        for b in range(1, n_attn):
            total = total + part_recv[b, other]
        totals.append(total)
    state = res_buf[...] + jnp.concatenate(
        [totals[other][xx * req : (xx + 1) * req] for xx in range(n_x) for other in range(CORES)],
        axis=0,
    )
    square = jnp.sum((state * state).T, axis=0, keepdims=True)
    pieces = split3(square)
    place = lax.broadcasted_iota(jnp.int32, (CAP, block), 0) - PARTS * a
    extra = jnp.zeros((CAP, block), F32)
    for p in range(PARTS):
        extra = extra + jnp.where(place == p, pieces[p].astype(F32), 0.0)
    normed[a, :block, :] = (state * gain_buf[...]).astype(BF16)
    normed[a, block:, :] = extra.astype(BF16)

    def push_norm(i):
        return pltpu.make_async_remote_copy(
            src_ref=normed.at[a],
            dst_ref=normed.at[a],
            send_sem=norm_send.at[i],
            recv_sem=norm_recv.at[a],
            device_id=(wrap(a + i, n_attn), e),
            device_id_type=MESH,
        )

    for i in range(1, n_attn):
        push_norm(i).start()

    squares = jnp.zeros((slots, HD), F32)
    blank = jnp.zeros((HD - CAP, block), F32)
    for i in range(n_attn):
        b = wrap(a + i, n_attn)
        if i > 0:
            pltpu.make_async_copy(normed.at[b], normed.at[b], norm_recv.at[b]).wait()
        beside = jnp.concatenate([normed[b, block:, :].astype(F32), blank], axis=0).T
        both = jnp.concatenate([normed[b, :block, :], beside.astype(BF16)], axis=1)
        picked = dot(select[b], both)
        x_send[:, b] = picked[:, :HD].astype(BF16).reshape(n_exp, CAP, HD)
        squares = squares + picked[:, HD:]
    x_send[:, n_attn] = squares.astype(BF16).reshape(n_exp, CAP, HD)

    def push_x(d):
        to = wrap(e + d, n_exp)
        return pltpu.make_async_remote_copy(
            src_ref=x_send.at[to],
            dst_ref=x_recv.at[e],
            send_sem=xs_sem.at[d],
            recv_sem=xr_sem.at[e],
            device_id=(a, to),
            device_id_type=MESH,
        )

    def start_x(d, carry):
        push_x(d).start()
        return carry

    lax.fori_loop(1, n_exp, start_x, 0)
    x_recv[e] = x_send[e]

    for i in range(n_z):
        zz = wrap(z + i, n_z)
        for q in range(per_z):
            source = zz * per_z + q

            def arrived(source=source):
                pltpu.make_async_copy(
                    x_recv.at[source], x_recv.at[source], xr_sem.at[source]
                ).wait()

            if i > 0:
                arrived()
            else:
                pl.when(source != e)(arrived)
        load_gate_up(zz).wait()
        left = jnp.concatenate(
            [x_recv[zz * per_z + q, :n_attn].reshape(rows, HD) for q in range(per_z)], axis=1
        )
        product = dot(left, gate_up_buf[pl.ds(pl.multiple_of(zz * depth, depth), depth), :])
        if i == 0:
            mixed[...] = product
        else:
            mixed[...] += product

    total = jnp.zeros((CAP, HD), F32)
    for source in range(n_exp):
        total = total + x_recv[source, n_attn].astype(F32)
    scale = jnp.concatenate(
        [
            lax.rsqrt(
                jnp.sum(total[:, PARTS * b : PARTS * (b + 1)], axis=1, keepdims=True) / features
                + 1e-06
            )
            for b in range(n_attn)
        ],
        axis=0,
    )
    gate = mixed[:, :width] * scale
    up = mixed[:, width:] * scale
    inner = (gate / (1.0 + jnp.exp(-gate)) * up).astype(BF16)

    load_down.wait()

    def push_y(to):
        return pltpu.make_async_remote_copy(
            src_ref=y_send.at[to],
            dst_ref=y_recv.at[e],
            send_sem=ys_sem.at[to],
            recv_sem=yr_sem.at[e],
            device_id=(a, to),
            device_id_type=MESH,
        )

    for i in [*range(1, n_z), 0]:
        zz = wrap(z + i, n_z)
        produced = dot(
            inner, down_buf[:, pl.ds(pl.multiple_of(zz * depth, depth), depth)]
        ).astype(BF16)
        for q in range(per_z):
            to = zz * per_z + q
            y_send[to] = produced[:, q * HD : (q + 1) * HD].reshape(n_attn, CAP, HD)

            def leave(to=to):
                push_y(to).start()

            if i > 0:
                leave()
            else:
                pl.when(to != e)(leave)
    y_recv[e] = y_send[e]

    for source in range(n_exp):
        @pl.when(e != source)
        def _():
            pltpu.make_async_copy(
                y_recv.at[source], y_recv.at[source], yr_sem.at[source]
            ).wait()

    def push_moe(i):
        return pltpu.make_async_remote_copy(
            src_ref=moe_send.at[i],
            dst_ref=moe_recv.at[a],
            send_sem=ms_sem.at[i],
            recv_sem=mr_sem.at[a],
            device_id=(wrap(a + i, n_attn), e),
            device_id_type=MESH,
        )

    for i in [*range(1, n_attn), 0]:
        b = wrap(a + i, n_attn)
        back = y_recv[:, b].reshape(slots, HD)
        share = dot(comb_high[b], back) + dot(comb_low[b], back)
        if i > 0:
            moe_send[i] = share
            push_moe(i).start()
        else:
            state = state + share
    for i in range(1, n_attn):
        b = wrap(a + i, n_attn)
        pltpu.make_async_copy(moe_recv.at[b], moe_recv.at[b], mr_sem.at[b]).wait()
        state = state + moe_recv[b]
    out[...] = state

    def end_att(d, carry):
        push_att(d).wait_send()
        return carry

    lax.fori_loop(1, chips, end_att, 0)

    def end_x(d, carry):
        push_x(d).wait_send()
        return carry

    lax.fori_loop(1, n_exp, end_x, 0)

    def end_y(d, carry):
        push_y(wrap(e + d, n_exp)).wait_send()
        return carry

    lax.fori_loop(1, n_exp, end_y, 0)
    push_w.wait_send()
    for i in range(1, n_attn):
        push_ids(i).wait_send()
        push_gates(i).wait_send()
        push_norm(i).wait_send()
        push_moe(i).wait_send()
        for other in range(CORES):
            push_part(i, other).wait_send()
    push_part(0, 1 - core).wait_send()


def body(
    n_attn,
    n_exp,
    residual,
    queries,
    keys,
    values,
    lengths,
    out_weight,
    norm_gain,
    expert_ids,
    gates,
    gate_up,
    down,
):
    req, span = keys.shape[0], keys.shape[1]
    heads = queries.shape[1] // HD
    width = down.shape[1]
    features = gate_up.shape[1]
    block = residual.shape[0]
    n_z = n_attn
    n_x = n_exp // (CORES * n_z)
    rows = n_attn * CAP
    slots = n_exp * CAP
    half = n_x * req
    groups = 4
    top = expert_ids.shape[1]
    cfg = (n_attn, n_z, n_x, req, heads, width)
    anywhere = pl.BlockSpec(memory_space=pl.ANY)
    vmem = pltpu.VMEM
    sem = pltpu.SemaphoreType.DMA
    return pl.pallas_call(
        functools.partial(layer_kernel, cfg),
        out_shape=jax.ShapeDtypeStruct(residual.shape, F32),
        in_specs=[pl.BlockSpec(memory_space=pltpu.SMEM)] + [anywhere] * 10,
        out_specs=pl.BlockSpec(memory_space=pltpu.VMEM),
        scratch_shapes=[
            vmem(queries.shape, BF16),
            vmem((req * heads, HD), BF16),
            vmem((req * heads, HD), BF16),
            vmem(keys.shape, BF16),
            vmem(values.shape, BF16),
            vmem((heads * HD, CORES * HD), BF16),
            vmem(residual.shape, F32),
            vmem((1, HD), F32),
            vmem((n_attn, top, block), jnp.int32),
            vmem((n_attn, top, block), F32),
            vmem((n_z, n_x, heads, req, HD), BF16),
            vmem((n_attn, CORES, half, HD), F32),
            vmem((n_attn, CORES, half, HD), F32),
            vmem((n_attn, block + CAP, HD), BF16),
            vmem((n_attn, slots, block), BF16),
            vmem((n_attn, block, slots), BF16),
            vmem((n_attn, block, slots), BF16),
            vmem((n_exp, n_attn + 1, CAP, HD), BF16),
            vmem((n_exp, n_attn + 1, CAP, HD), BF16),
            vmem((features, 2 * width), BF16),
            vmem((width, features), BF16),
            vmem((rows, 2 * width), F32),
            vmem((n_exp, n_attn, CAP, HD), BF16),
            vmem((n_exp, n_attn, CAP, HD), BF16),
            vmem((n_attn, block, HD), F32),
            vmem((n_attn, block, HD), F32),
            sem((8,)),
            sem((groups,)),
            sem((groups,)),
            sem((n_z,)),
            sem,
            sem,
            sem((n_attn,)),
            sem((n_attn,)),
            sem((n_attn,)),
            sem((n_attn,)),
            sem((n_z * n_x,)),
            sem((n_z * n_x,)),
            sem((n_attn * CORES,)),
            sem((n_attn * CORES,)),
            sem((n_attn,)),
            sem((n_attn,)),
            sem((n_exp,)),
            sem((n_exp,)),
            sem((n_exp,)),
            sem((n_exp,)),
            sem((n_attn,)),
            sem((n_attn,)),
        ],
        compiler_params=pltpu.CompilerParams(
            collective_id=0, has_side_effects=True, vmem_limit_bytes=58 * 1024 * 1024
        ),
        name="layer",
    )(
        lengths,
        residual,
        queries,
        keys,
        values,
        out_weight,
        norm_gain.reshape(1, HD),
        expert_ids.T,
        gates.T,
        gate_up,
        down,
    )


def solution(mesh):
    in_specs = (
        P("attn", "expert"),
        P("expert", "attn"),
        P("expert", None, "attn"),
        P("expert", None, "attn"),
        P("expert"),
        P("attn", "expert"),
        P("expert"),
        P("attn", None),
        P("attn", None),
        P(("attn", "expert"), None, None),
        P(("attn", "expert"), None, None),
    )
    run = functools.partial(body, mesh.shape["attn"], mesh.shape["expert"])
    return jax.shard_map(
        run, mesh=mesh, in_specs=in_specs, out_specs=P("attn", "expert"), check_vma=False
    )
```

```python
import functools
import math

import jax
import jax.numpy as jnp
from jax import lax
from jax.experimental import pallas as pl
from jax.experimental.pallas import tpu as pltpu
from jax.sharding import PartitionSpec as P

HD = 128
CAP = 16
CORES = 2
F32 = jnp.float32
BF16 = jnp.bfloat16
MESH = pl.DeviceIdType.MESH
NT = (((1,), (1,)), ((), ()))


def dot(left, right):
    return jnp.dot(left, right, preferred_element_type=F32)


def dot_nt(left, right):
    return lax.dot_general(left, right, NT, preferred_element_type=F32)


def layer_kernel(
    cfg,
    lengths,
    residual,
    queries,
    keys,
    values,
    out_weight,
    gain,
    ids,
    gates,
    gate_up,
    down,
    out,
    q_in,
    q_rows,
    o_rows,
    k_buf,
    v_buf,
    w_buf,
    res_buf,
    gain_all,
    gain_inv,
    ids_buf,
    gates_buf,
    att,
    part_send,
    part_recv,
    select,
    comb_high,
    comb_low,
    x_send,
    x_recv,
    gate_up_buf,
    down_buf,
    mixed,
    y_send,
    y_recv,
    in_sem,
    k_sem,
    v_sem,
    gate_sem,
    w_send,
    w_recv,
    gain_send,
    gain_recv,
    own_send,
    pass_send,
    att_recv,
    rs_send,
    rs_recv,
    xs_sem,
    xr_sem,
    ys_sem,
    yr_sem,
):
    n_attn, n_z, n_x, req, heads, width = cfg
    n_exp = n_z * n_x * CORES
    per_z = n_x * CORES
    block = per_z * req
    half = n_x * req
    features = n_exp * HD
    slots = n_exp * CAP
    rows = n_attn * CAP
    experts = n_attn * n_exp
    split = heads // 2
    a = lax.axis_index("attn")
    e = lax.axis_index("expert")
    core = lax.rem(e, CORES)
    chip = lax.div(e, CORES)
    x = lax.rem(chip, n_x)
    z = lax.div(chip, n_x)
    sibling = chip * CORES + (1 - core)
    mine = a * n_exp + e

    def wrap(value, size):
        return lax.rem(value, size)

    def ring(size):
        return sorted(range(1, size), key=lambda d: min(d, size - d))

    n_group = k_sem.shape[0]
    group = req // n_group
    load_q = pltpu.make_async_copy(queries, q_in, in_sem.at[0])
    load_q.start()

    def load_k(g):
        span = pl.ds(g * group, group)
        return pltpu.make_async_copy(keys.at[span], k_buf.at[span], k_sem.at[g])

    def load_v(g):
        span = pl.ds(g * group, group)
        return pltpu.make_async_copy(values.at[span], v_buf.at[span], v_sem.at[g])

    for g in range(n_group):
        load_k(g).start()
        load_v(g).start()
    own_columns = pl.ds(pl.multiple_of(core * HD, HD), HD)
    load_w = pltpu.make_async_copy(out_weight, w_buf.at[:, own_columns], in_sem.at[1])
    load_res = pltpu.make_async_copy(residual, res_buf, in_sem.at[2])
    load_ids = pltpu.make_async_copy(ids, ids_buf, in_sem.at[3])
    load_gates = pltpu.make_async_copy(gates, gates_buf, in_sem.at[4])
    for load in (load_w, load_res, load_ids, load_gates):
        load.start()

    barrier = pltpu.get_barrier_semaphore()

    def greet(d, carry):
        pl.semaphore_signal(
            barrier, inc=1, device_id=(a, wrap(e + d, n_exp)), device_id_type=MESH
        )
        return carry

    lax.fori_loop(1, n_exp, greet, 0)
    for i in range(1, n_attn):
        for other in range(CORES):
            pl.semaphore_signal(
                barrier,
                inc=1,
                device_id=(wrap(a + i, n_attn), chip * CORES + other),
                device_id_type=MESH,
            )

    load_q.wait()
    pairs = (heads * req, heads * req)
    first = lax.broadcasted_iota(jnp.int32, pairs, 0)
    second = lax.broadcasted_iota(jnp.int32, pairs, 1)
    by_request = (lax.div(first, heads) == lax.rem(second, req)) & (
        lax.rem(first, heads) == lax.div(second, req)
    )
    stacked = jnp.concatenate([q_in[:, h * HD : (h + 1) * HD] for h in range(heads)], axis=0)
    q_rows[...] = dot(by_request.astype(F32).astype(BF16), stacked).astype(BF16)
    span = k_buf.shape[1]
    position = lax.broadcasted_iota(jnp.int32, (heads, span), 1)

    def score(g):
        load_k(g).wait()
        return [
            dot_nt(q_rows[i * heads : (i + 1) * heads, :], k_buf[i])
            for i in range(g * group, (g + 1) * group)
        ]

    ahead = score(0)
    for g in range(n_group):
        scores = ahead
        if g + 1 < n_group:
            ahead = score(g + 1)
        weights = []
        for j in range(group):
            masked = jnp.where(
                position < lengths[g * group + j], scores[j] * (1.0 / math.sqrt(HD)), -1e30
            )
            expo = jnp.exp(masked - jnp.max(masked, axis=1, keepdims=True))
            weights.append((expo / jnp.sum(expo, axis=1, keepdims=True)).astype(BF16))
        load_v(g).wait()
        results = [dot(weights[j], v_buf[g * group + j]).astype(BF16) for j in range(group)]
        o_rows[g * group * heads : (g + 1) * group * heads, :] = jnp.concatenate(results, axis=0)
    by_head = (lax.div(first, req) == lax.rem(second, heads)) & (
        lax.rem(first, req) == lax.div(second, heads)
    )
    own = dot(by_head.astype(F32).astype(BF16), o_rows[...]).astype(BF16)
    for part in range(2):
        att[part, z, x] = own[part * split * req : (part + 1) * split * req].reshape(
            split, req, HD
        )

    pl.semaphore_wait(barrier, n_exp - 1 + CORES * (n_attn - 1))

    def along_x(part, item_z, item_x, d, sem):
        return pltpu.make_async_remote_copy(
            src_ref=att.at[part, item_z, item_x],
            dst_ref=att.at[part, item_z, item_x],
            send_sem=sem,
            recv_sem=att_recv.at[part, item_z, item_x],
            device_id=(a, (z * n_x + wrap(x + d, n_x)) * CORES + core),
            device_id_type=MESH,
        )

    def along_z(part, item_z, item_x, d, sem):
        return pltpu.make_async_remote_copy(
            src_ref=att.at[part, item_z, item_x],
            dst_ref=att.at[part, item_z, item_x],
            send_sem=sem,
            recv_sem=att_recv.at[part, item_z, item_x],
            device_id=(a, (wrap(z + d, n_z) * n_x + x) * CORES + core),
            device_id_type=MESH,
        )

    def att_arrived(part, item_z, item_x):
        item = att.at[part, item_z, item_x]
        pltpu.make_async_copy(item, item, att_recv.at[part, item_z, item_x]).wait()

    sends = []
    for part in (0, 1):
        for k, d in enumerate(ring(n_x)):
            sends.append(("x", part, k, d))
        for k, d in enumerate(ring(n_z)):
            sends.append(("z", part, k, d))
    order = [c for c in sends if (c[0] == "x") == (c[1] == 0)]
    order += [c for c in sends if (c[0] == "x") != (c[1] == 0)]

    def own_copy(c):
        axis, part, k, d = c
        if axis == "x":
            return along_x(part, z, x, d, own_send.at[part, k])
        return along_z(part, z, x, d, own_send.at[part, n_x - 1 + k])

    for c in order:
        own_copy(c).start()

    push_w = pltpu.make_async_remote_copy(
        src_ref=out_weight,
        dst_ref=w_buf.at[:, own_columns],
        send_sem=w_send,
        recv_sem=w_recv,
        device_id=(a, sibling),
        device_id_type=MESH,
    )
    push_w.start()

    depth = per_z * HD

    def load_gate_up(g):
        part = pl.ds(pl.multiple_of(g * depth, depth), depth)
        return pltpu.make_async_copy(
            gate_up.at[0, part, :], gate_up_buf.at[part, :], gate_sem.at[g]
        )

    load_down = pltpu.make_async_copy(down.at[0], down_buf, in_sem.at[5])
    for g in range(n_z):
        load_gate_up(g).start()
    load_down.start()

    own_gain = pltpu.make_async_copy(gain, gain_all.at[e], gain_recv)
    own_gain.start()

    def push_gain(d):
        return pltpu.make_async_remote_copy(
            src_ref=gain,
            dst_ref=gain_all.at[e],
            send_sem=gain_send.at[d],
            recv_sem=gain_recv,
            device_id=(a, wrap(e + d, n_exp)),
            device_id_type=MESH,
        )

    def start_gain(d, carry):
        push_gain(d).start()
        return carry

    lax.fori_loop(1, n_exp, start_gain, 0)

    passes = []
    for k in range(max(n_x, n_z) - 1):
        if k < n_x - 1:
            from_x = wrap(x + ring(n_x)[k], n_x)
            att_arrived(0, z, from_x)
            for m, d in enumerate(ring(n_z)):
                copy = along_z(0, z, from_x, d, pass_send.at[0, k, m])
                copy.start()
                passes.append(copy)
        if k < n_z - 1:
            from_z = wrap(z + ring(n_z)[k], n_z)
            att_arrived(1, from_z, x)
            for m, d in enumerate(ring(n_x)):
                copy = along_x(1, from_z, x, d, pass_send.at[1, k, m])
                copy.start()
                passes.append(copy)

    load_ids.wait()
    load_gates.wait()
    earlier = (
        lax.broadcasted_iota(jnp.int32, (block, block), 0)
        < lax.broadcasted_iota(jnp.int32, (block, block), 1)
    ).astype(F32).astype(BF16)
    spread_row = lax.broadcasted_iota(jnp.int32, (slots, n_exp), 0)
    spread_col = lax.broadcasted_iota(jnp.int32, (slots, n_exp), 1)
    spread = (
        ((spread_row >= spread_col * CAP) & (spread_row < (spread_col + 1) * CAP))
        .astype(F32)
        .astype(BF16)
    )
    slot = lax.rem(lax.broadcasted_iota(jnp.int32, (slots, block), 0), CAP).astype(F32)
    local = lax.broadcasted_iota(jnp.int32, (n_exp, block), 0)
    for p in range(n_attn):
        named = local + p * n_exp
        chosen = jnp.zeros((n_exp, block), F32)
        weight = jnp.zeros((n_exp, block), F32)
        for k in range(ids_buf.shape[0]):
            hit = ids_buf[k : k + 1, :] == named
            chosen = chosen + jnp.where(hit, 1.0, 0.0)
            weight = weight + jnp.where(hit, gates_buf[k : k + 1, :], 0.0)
        rank = dot(chosen.astype(BF16), earlier)
        high = weight.astype(BF16)
        low = (weight - high.astype(F32)).astype(BF16)
        table = jnp.concatenate([rank.astype(BF16), chosen.astype(BF16), high, low], axis=1)
        wide = dot(spread, table)
        here = wide[:, :block] == slot
        select[p] = jnp.where(here, wide[:, block : 2 * block], 0.0).astype(BF16)
        comb_high[p] = jnp.where(here, wide[:, 2 * block : 3 * block], 0.0).T.astype(BF16)
        comb_low[p] = jnp.where(here, wide[:, 3 * block :], 0.0).T.astype(BF16)

    pltpu.make_async_copy(gain_all, gain_all, gain_recv).wait()
    gain_inv[...] = 1.0 / gain_all[...]

    load_w.wait()
    push_w.wait_recv()

    def push_part(b, other):
        return pltpu.make_async_remote_copy(
            src_ref=part_send.at[b, other],
            dst_ref=part_recv.at[a, core],
            send_sem=rs_send.at[b * CORES + other],
            recv_sem=rs_recv.at[a * CORES + core],
            device_id=(b, chip * CORES + other),
            device_id_type=MESH,
        )

    for i in [0, *ring(n_z)]:
        b = wrap(z + i, n_z)
        for d in ring(n_x):
            if i > 0:
                att_arrived(0, b, wrap(x + d, n_x))
            att_arrived(1, b, wrap(x + d, n_x))
        if i > 0:
            att_arrived(0, b, x)
        left = jnp.concatenate(
            [att[h // split, b, :, h % split].reshape(half, HD) for h in range(heads)], axis=1
        )
        product = dot(left, w_buf[...])
        for other in range(CORES):
            part_send[b, other] = product[:, other * HD : (other + 1) * HD].astype(BF16)

        @pl.when(b != a)
        def _():
            for other in range(CORES):
                push_part(b, other).start()

        @pl.when(b == a)
        def _():
            push_part(b, 1 - core).start()
            part_recv[a, core] = part_send[b, core]

    for i in range(n_attn):
        b = wrap(a + i, n_attn)
        for other in range(CORES):
            def arrived(b=b, other=other):
                pltpu.make_async_copy(
                    part_recv.at[b, other],
                    part_recv.at[b, other],
                    rs_recv.at[b * CORES + other],
                ).wait()

            if i > 0:
                arrived()
            else:
                pl.when(core != other)(arrived)

    load_res.wait()
    totals = []
    for other in range(CORES):
        total = part_recv[0, other].astype(F32)
        for b in range(1, n_attn):
            total = total + part_recv[b, other].astype(F32)
        totals.append(total)
    state = res_buf[...] + jnp.concatenate(
        [totals[other][xx * req : (xx + 1) * req] for xx in range(n_x) for other in range(CORES)],
        axis=0,
    )
    out[...] = state
    scaled = (state * gain_all[e]).astype(BF16)

    for p in range(n_attn):
        picked = dot(select[p], scaled).astype(BF16)
        x_send[p * n_exp : (p + 1) * n_exp] = picked.reshape(n_exp, CAP, HD)

    def push_x(to_a, to_e):
        return pltpu.make_async_remote_copy(
            src_ref=x_send.at[to_a * n_exp + to_e],
            dst_ref=x_recv.at[e, a],
            send_sem=xs_sem,
            recv_sem=xr_sem.at[z],
            device_id=(to_a, to_e),
            device_id_type=MESH,
        )

    own_x = pltpu.make_async_copy(x_send.at[mine], x_recv.at[e, a], xr_sem.at[z])
    own_x.start()

    def start_x(d, carry):
        for i in [*range(1, n_attn), 0]:
            push_x(wrap(a + i, n_attn), wrap(e + d, n_exp)).start()
        return carry

    lax.fori_loop(1, n_exp, start_x, 0)
    for i in range(1, n_attn):
        push_x(wrap(a + i, n_attn), e).start()

    squares = jnp.zeros((rows, HD), F32)
    for i in [0, *ring(n_z)]:
        zz = wrap(z + i, n_z)
        arrived = x_recv.at[pl.ds(zz * per_z, per_z)]
        pltpu.make_async_copy(arrived, arrived, xr_sem.at[zz]).wait()
        load_gate_up(zz).wait()
        pieces = [x_recv[zz * per_z + q].reshape(rows, HD) for q in range(per_z)]
        for q in range(per_z):
            plain = pieces[q].astype(F32) * gain_inv[zz * per_z + q]
            squares = squares + plain * plain
        left = jnp.concatenate(pieces, axis=1)
        product = dot(left, gate_up_buf[pl.ds(pl.multiple_of(zz * depth, depth), depth), :])
        if i == 0:
            mixed[...] = product
        else:
            mixed[...] += product

    scale = lax.rsqrt(jnp.sum(squares, axis=1, keepdims=True) / features + 1e-06)
    gate = mixed[:, :width] * scale
    up = mixed[:, width:] * scale
    inner = (gate / (1.0 + jnp.exp(-gate)) * up).astype(BF16)

    load_down.wait()

    def push_y(to_a, to_e):
        return pltpu.make_async_remote_copy(
            src_ref=y_send.at[to_e * n_attn + to_a],
            dst_ref=y_recv.at[mine],
            send_sem=ys_sem,
            recv_sem=yr_sem.at[a],
            device_id=(to_a, to_e),
            device_id_type=MESH,
        )

    for i in [*ring(n_z)[::-1], 0]:
        zz = wrap(z + i, n_z)
        produced = dot(
            inner, down_buf[:, pl.ds(pl.multiple_of(zz * depth, depth), depth)]
        ).astype(BF16)
        for q in range(per_z):
            y_send[pl.ds((zz * per_z + q) * n_attn, n_attn)] = produced[
                :, q * HD : (q + 1) * HD
            ].reshape(n_attn, CAP, HD)

        def start_y(q, carry, zz=zz, own=(i == 0)):
            to = zz * per_z + q
            for k in range(1, n_attn):
                push_y(wrap(a + k, n_attn), to).start()
            if own:
                pl.when(to != e)(lambda: push_y(a, to).start())
            else:
                push_y(a, to).start()
            return carry

        lax.fori_loop(0, per_z, start_y, 0)
    own_y = pltpu.make_async_copy(y_send.at[e * n_attn + a], y_recv.at[mine], yr_sem.at[a])
    own_y.start()

    for i in range(n_attn):
        p = wrap(a + i, n_attn)
        arrived = y_recv.at[pl.ds(p * n_exp, n_exp)]
        pltpu.make_async_copy(arrived, arrived, yr_sem.at[p]).wait()
        back = y_recv[pl.ds(p * n_exp, n_exp)].reshape(slots, HD)
        out[...] += dot(comb_high[p], back) + dot(comb_low[p], back)

    for c in order:
        own_copy(c).wait_send()
    for copy in passes:
        copy.wait_send()
    push_w.wait_send()

    def end_gain(d, carry):
        push_gain(d).wait_send()
        return carry

    lax.fori_loop(1, n_exp, end_gain, 0)
    for b in range(n_attn):
        for other in range(CORES):
            def left_here(b=b, other=other):
                push_part(b, other).wait_send()

            pl.when(jnp.logical_not((b == a) & (core == other)))(left_here)
    for buffer, sem in ((x_send, xs_sem), (y_send, ys_sem)):
        gone = buffer.at[pl.ds(0, experts - 1)]
        pltpu.make_async_copy(gone, gone, sem).wait()


def body(
    n_attn,
    n_exp,
    residual,
    queries,
    keys,
    values,
    lengths,
    out_weight,
    norm_gain,
    expert_ids,
    gates,
    gate_up,
    down,
):
    req, span = keys.shape[0], keys.shape[1]
    heads = queries.shape[1] // HD
    width = down.shape[1]
    features = gate_up.shape[1]
    block = residual.shape[0]
    n_z = n_attn
    n_x = n_exp // (CORES * n_z)
    rows = n_attn * CAP
    slots = n_exp * CAP
    half = n_x * req
    groups = 4
    top = expert_ids.shape[1]
    cfg = (n_attn, n_z, n_x, req, heads, width)
    anywhere = pl.BlockSpec(memory_space=pl.ANY)
    vmem = pltpu.VMEM
    sem = pltpu.SemaphoreType.DMA
    return pl.pallas_call(
        functools.partial(layer_kernel, cfg),
        out_shape=jax.ShapeDtypeStruct(residual.shape, F32),
        in_specs=[pl.BlockSpec(memory_space=pltpu.SMEM)] + [anywhere] * 10,
        out_specs=pl.BlockSpec(memory_space=pltpu.VMEM),
        scratch_shapes=[
            vmem(queries.shape, BF16),
            vmem((req * heads, HD), BF16),
            vmem((req * heads, HD), BF16),
            vmem(keys.shape, BF16),
            vmem(values.shape, BF16),
            vmem((heads * HD, CORES * HD), BF16),
            vmem(residual.shape, F32),
            vmem((n_exp, 1, HD), F32),
            vmem((n_exp, 1, HD), F32),
            vmem((top, block), jnp.int32),
            vmem((top, block), F32),
            vmem((2, n_z, n_x, heads // 2, req, HD), BF16),
            vmem((n_attn, CORES, half, HD), BF16),
            vmem((n_attn, CORES, half, HD), BF16),
            vmem((n_attn, slots, block), BF16),
            vmem((n_attn, block, slots), BF16),
            vmem((n_attn, block, slots), BF16),
            vmem((n_attn * n_exp, CAP, HD), BF16),
            vmem((n_exp, n_attn, CAP, HD), BF16),
            vmem((features, 2 * width), BF16),
            vmem((width, features), BF16),
            vmem((rows, 2 * width), F32),
            vmem((n_exp * n_attn, CAP, HD), BF16),
            vmem((n_attn * n_exp, CAP, HD), BF16),
            sem((6,)),
            sem((groups,)),
            sem((groups,)),
            sem((n_z,)),
            sem,
            sem,
            sem((n_exp,)),
            sem,
            sem((2, n_x + n_z - 2)),
            sem((2, max(n_x, n_z) - 1, max(n_x, n_z) - 1)),
            sem((2, n_z, n_x)),
            sem((n_attn * CORES,)),
            sem((n_attn * CORES,)),
            sem,
            sem((n_z,)),
            sem,
            sem((n_attn,)),
        ],
        compiler_params=pltpu.CompilerParams(
            collective_id=0, has_side_effects=True, vmem_limit_bytes=58 * 1024 * 1024
        ),
        name="layer",
    )(
        lengths,
        residual,
        queries,
        keys,
        values,
        out_weight,
        norm_gain.reshape(1, HD),
        expert_ids.T,
        gates.T,
        gate_up,
        down,
    )


def solution(mesh):
    in_specs = (
        P("attn", "expert"),
        P("expert", "attn"),
        P("expert", None, "attn"),
        P("expert", None, "attn"),
        P("expert"),
        P("attn", "expert"),
        P("expert"),
        P("attn", None),
        P("attn", None),
        P(("attn", "expert"), None, None),
        P(("attn", "expert"), None, None),
    )
    run = functools.partial(body, mesh.shape["attn"], mesh.shape["expert"])
    return jax.shard_map(
        run, mesh=mesh, in_specs=in_specs, out_specs=P("attn", "expert"), check_vma=False
    )
```

```python
import functools
import math

import jax
import jax.numpy as jnp
from jax import lax
from jax.experimental import pallas as pl
from jax.experimental.pallas import tpu as pltpu
from jax.sharding import PartitionSpec as P

HD = 128
CAP = 16
CORES = 2
PARTS = 3
F32 = jnp.float32
BF16 = jnp.bfloat16
MESH = pl.DeviceIdType.MESH
NT = (((1,), (1,)), ((), ()))


def dot(left, right):
    return jnp.dot(left, right, preferred_element_type=F32)


def dot_nt(left, right):
    return lax.dot_general(left, right, NT, preferred_element_type=F32)


def layer_kernel(
    cfg,
    lengths,
    residual,
    queries,
    keys,
    values,
    out_weight,
    gain,
    ids,
    gates,
    gate_up,
    down,
    out,
    q_in,
    q_rows,
    o_rows,
    k_buf,
    v_buf,
    w_buf,
    res_buf,
    len_buf,
    gain_buf,
    gain_inv,
    ids_buf,
    gates_buf,
    att,
    part_send,
    part_recv,
    select,
    comb_high,
    comb_low,
    x_send,
    x_recv,
    gate_up_buf,
    down_buf,
    mixed,
    y_send,
    y_recv,
    in_sem,
    k_sem,
    v_sem,
    gate_sem,
    w_send,
    w_recv,
    gain_send,
    gain_recv,
    own_send,
    pass_send,
    att_recv,
    rs_send,
    rs_recv,
    xs_sem,
    xr_sem,
    ys_sem,
    yr_sem,
):
    n_attn, n_z, n_x, req, heads, width = cfg
    n_exp = n_z * n_x * CORES
    per_z = n_x * CORES
    block = per_z * req
    half = n_x * req
    features = n_exp * HD
    slots = n_exp * CAP
    rows = n_attn * CAP
    experts = n_attn * n_exp
    part_req = req // 2
    couples = heads // 2
    far = [n_z // 2, *(d for d in range(1, n_z) if d != n_z // 2), 0]
    a = lax.axis_index("attn")
    e = lax.axis_index("expert")
    core = lax.rem(e, CORES)
    chip = lax.div(e, CORES)
    x = lax.rem(chip, n_x)
    z = lax.div(chip, n_x)
    sibling = chip * CORES + (1 - core)
    lane = lax.rem(e, per_z)

    def wrap(value, size):
        return lax.rem(value, size)

    def ring(size):
        return sorted(range(1, size), key=lambda d: min(d, size - d))

    n_group = k_sem.shape[0]
    group = req // n_group
    load_q = pltpu.make_async_copy(queries, q_in, in_sem.at[8])
    load_len = pltpu.make_async_copy(lengths, len_buf, in_sem.at[6])
    load_q.start()
    load_len.start()

    def load_k(g):
        span = pl.ds(g * group, group)
        return pltpu.make_async_copy(keys.at[span], k_buf.at[span], k_sem.at[g])

    def load_v(g):
        span = pl.ds(g * group, group)
        return pltpu.make_async_copy(values.at[span], v_buf.at[span], v_sem.at[g])

    for g in range(n_group):
        load_k(g).start()
        load_v(g).start()

    def load_w(q):
        return pltpu.make_async_copy(out_weight.at[:, q], w_buf.at[q, core], in_sem.at[q])

    load_gain = pltpu.make_async_copy(gain, gain_buf, in_sem.at[7])
    load_res = pltpu.make_async_copy(residual, res_buf, in_sem.at[2])
    load_ids = pltpu.make_async_copy(ids, ids_buf, in_sem.at[3])
    load_gates = pltpu.make_async_copy(gates, gates_buf, in_sem.at[4])
    for load in (load_gain, load_res, load_ids, load_gates, load_w(0), load_w(1)):
        load.start()

    barrier = pltpu.get_barrier_semaphore()
    known = [(a, (z * n_x + wrap(x + d, n_x)) * CORES + core) for d in range(1, n_x)]
    known += [(a, (wrap(z + d, n_z) * n_x + x) * CORES + core) for d in range(1, n_z)]
    known += [(a, sibling)]
    known += [
        (wrap(a + i, n_attn), chip * CORES + other)
        for i in range(1, n_attn)
        for other in range(CORES)
    ]
    for device in known:
        pl.semaphore_signal(barrier, inc=1, device_id=device, device_id_type=MESH)

    load_q.wait()
    load_len.wait()
    pairs = (heads * req, heads * req)
    first = lax.broadcasted_iota(jnp.int32, pairs, 0)
    second = lax.broadcasted_iota(jnp.int32, pairs, 1)
    by_request = (lax.div(first, heads) == lax.rem(second, req)) & (
        lax.rem(first, heads) == lax.div(second, req)
    )
    stacked = jnp.concatenate([q_in[:, h * HD : (h + 1) * HD] for h in range(heads)], axis=0)
    q_rows[...] = dot(by_request.astype(F32).astype(BF16), stacked).astype(BF16)
    span = k_buf.shape[1]
    position = lax.broadcasted_iota(jnp.int32, (heads, span), 1)

    def score(g):
        load_k(g).wait()
        return [
            dot_nt(q_rows[i * heads : (i + 1) * heads, :], k_buf[i])
            for i in range(g * group, (g + 1) * group)
        ]

    def along_x(part, item_z, item_x, d, sem):
        item = att.at[part, item_z, item_x, pl.ds(0, couples + 1 - part)]
        return pltpu.make_async_remote_copy(
            src_ref=item,
            dst_ref=item,
            send_sem=sem,
            recv_sem=att_recv.at[part, item_z, item_x],
            device_id=(a, (z * n_x + wrap(x + d, n_x)) * CORES + core),
            device_id_type=MESH,
        )

    def along_z(part, item_z, item_x, d, sem):
        item = att.at[part, item_z, item_x, pl.ds(0, couples + 1 - part)]
        return pltpu.make_async_remote_copy(
            src_ref=item,
            dst_ref=item,
            send_sem=sem,
            recv_sem=att_recv.at[part, item_z, item_x],
            device_id=(a, (wrap(z + d, n_z) * n_x + x) * CORES + core),
            device_id_type=MESH,
        )

    def att_arrived(part, item_z, item_x):
        item = att.at[part, item_z, item_x, pl.ds(0, couples + 1 - part)]
        pltpu.make_async_copy(item, item, att_recv.at[part, item_z, item_x]).wait()

    sent = []
    mesh_pairs = (heads * part_req, heads * part_req)
    to_row = lax.broadcasted_iota(jnp.int32, mesh_pairs, 0)
    from_row = lax.broadcasted_iota(jnp.int32, mesh_pairs, 1)
    by_head = (
        (lax.div(from_row, heads) == lax.rem(to_row, part_req))
        & (lax.rem(from_row, heads) == lax.div(to_row, part_req))
    ).astype(F32).astype(BF16)

    def leave(part):
        span = heads * part_req
        own = dot(by_head, o_rows[part * span : (part + 1) * span, :]).astype(BF16)
        att[part, z, x, :couples] = own.reshape(couples, 2 * part_req, HD)
        if part == 0:
            load_gain.wait()
            place = lax.broadcasted_iota(jnp.int32, (2 * part_req, HD), 0)
            rest = gain_buf[...]
            tile = jnp.zeros((2 * part_req, HD), F32)
            for k in range(PARTS):
                piece = rest.astype(BF16).astype(F32)
                tile = tile + jnp.where(place == k, piece, 0.0)
                rest = rest - piece
            att[0, z, x, couples] = tile.astype(BF16)
            pl.semaphore_wait(barrier, len(known))
        steps = [(along_x, n_x), (along_z, n_z)]
        if part == 1:
            steps = steps[::-1]
        for k, (along, size) in enumerate(steps):
            for m, d in enumerate(ring(size)):
                copy = along(part, z, x, d, own_send.at[part, k, m])
                copy.start()
                sent.append(copy)

    ahead = score(0)
    for g in range(n_group):
        scores = ahead
        if g + 1 < n_group:
            ahead = score(g + 1)
        weights = []
        for j in range(group):
            masked = jnp.where(
                position < len_buf[g * group + j], scores[j] * (1.0 / math.sqrt(HD)), -1e30
            )
            expo = jnp.exp(masked - jnp.max(masked, axis=1, keepdims=True))
            weights.append((expo / jnp.sum(expo, axis=1, keepdims=True)).astype(BF16))
        load_v(g).wait()
        results = [dot(weights[j], v_buf[g * group + j]).astype(BF16) for j in range(group)]
        o_rows[g * group * heads : (g + 1) * group * heads, :] = jnp.concatenate(results, axis=0)
        if (g + 1) % (n_group // 2) == 0:
            leave(2 * g // n_group)

    def push_w(q):
        return pltpu.make_async_remote_copy(
            src_ref=out_weight.at[:, q],
            dst_ref=w_buf.at[q, core],
            send_sem=w_send.at[q],
            recv_sem=w_recv.at[q],
            device_id=(a, sibling),
            device_id_type=MESH,
        )

    for q in range(2):
        push_w(q).start()

    for k in range(max(n_x, n_z) - 1):
        if k < n_x - 1:
            from_x = wrap(x + ring(n_x)[k], n_x)
            att_arrived(0, z, from_x)
            for m, d in enumerate(ring(n_z)):
                copy = along_z(0, z, from_x, d, pass_send.at[0, k, m])
                copy.start()
                sent.append(copy)
        if k < n_z - 1:
            from_z = wrap(z + ring(n_z)[k], n_z)
            att_arrived(1, from_z, x)
            for m, d in enumerate(ring(n_x)):
                copy = along_x(1, from_z, x, d, pass_send.at[1, k, m])
                copy.start()
                sent.append(copy)

    depth = per_z * HD

    def load_gate_up(g):
        part = pl.ds(pl.multiple_of(g * depth, depth), depth)
        return pltpu.make_async_copy(
            gate_up.at[0, part, :], gate_up_buf.at[part, :], gate_sem.at[g]
        )

    load_down = pltpu.make_async_copy(down.at[0], down_buf, in_sem.at[5])
    for g in range(n_z):
        load_gate_up(g).start()
    load_down.start()

    load_ids.wait()
    load_gates.wait()
    earlier = (
        lax.broadcasted_iota(jnp.int32, (block, block), 0)
        < lax.broadcasted_iota(jnp.int32, (block, block), 1)
    ).astype(F32).astype(BF16)
    spread_row = lax.broadcasted_iota(jnp.int32, (slots, n_exp), 0)
    spread_col = lax.broadcasted_iota(jnp.int32, (slots, n_exp), 1)
    spread = (
        ((spread_row >= spread_col * CAP) & (spread_row < (spread_col + 1) * CAP))
        .astype(F32)
        .astype(BF16)
    )
    slot = lax.rem(lax.broadcasted_iota(jnp.int32, (slots, block), 0), CAP).astype(F32)
    local = lax.broadcasted_iota(jnp.int32, (n_exp, block), 0)
    for p in range(n_z):
        named = lax.div(local, per_z) * n_exp + p * per_z + lax.rem(local, per_z)
        chosen = jnp.zeros((n_exp, block), F32)
        weight = jnp.zeros((n_exp, block), F32)
        for k in range(ids_buf.shape[0]):
            hit = ids_buf[k : k + 1, :] == named
            chosen = chosen + jnp.where(hit, 1.0, 0.0)
            weight = weight + jnp.where(hit, gates_buf[k : k + 1, :], 0.0)
        rank = dot(chosen.astype(BF16), earlier)
        high = weight.astype(BF16)
        low = (weight - high.astype(F32)).astype(BF16)
        table = jnp.concatenate([rank.astype(BF16), chosen.astype(BF16), high, low], axis=1)
        wide = dot(spread, table)
        here = wide[:, :block] == slot
        select[p] = jnp.where(here, wide[:, block : 2 * block], 0.0).astype(BF16)
        comb_high[p] = jnp.where(here, wide[:, 2 * block : 3 * block], 0.0).T.astype(BF16)
        comb_low[p] = jnp.where(here, wide[:, 3 * block :], 0.0).T.astype(BF16)

    for q in range(2):
        load_w(q).wait()
        push_w(q).wait_recv()
    right = jnp.concatenate(
        [
            w_buf[q, other].reshape(couples * HD, HD)
            for q in range(2)
            for other in range(CORES)
        ],
        axis=1,
    )

    def push_part(b, other):
        return pltpu.make_async_remote_copy(
            src_ref=part_send.at[b, other],
            dst_ref=part_recv.at[a, core],
            send_sem=rs_send.at[b * CORES + other],
            recv_sem=rs_recv.at[a * CORES + core],
            device_id=(b, chip * CORES + other),
            device_id_type=MESH,
        )

    for i in [0, *ring(n_z)]:
        b = wrap(z + i, n_z)
        for d in ring(n_x):
            if i > 0:
                att_arrived(0, b, wrap(x + d, n_x))
            att_arrived(1, b, wrap(x + d, n_x))
        if i > 0:
            att_arrived(0, b, x)
        left = jnp.concatenate(
            [att[:, b, :, k].reshape(2 * half, HD) for k in range(couples)], axis=1
        )
        wide = dot(left, right)
        pieces = []
        for xx in range(n_x):
            for part in range(2):
                top = (part * n_x + xx) * 2 * part_req
                pieces.append(
                    wide[top : top + part_req, : CORES * HD]
                    + wide[top + part_req : top + 2 * part_req, CORES * HD :]
                )
        product = jnp.concatenate(pieces, axis=0)
        for other in range(CORES):
            part_send[b, other] = product[:, other * HD : (other + 1) * HD].astype(BF16)

        @pl.when(b != a)
        def _():
            for other in range(CORES):
                push_part(b, other).start()

        @pl.when(b == a)
        def _():
            push_part(b, 1 - core).start()
            part_recv[a, core] = part_send[b, core]

    for k in range(n_z * n_x):
        tile = att[0, k // n_x, k % n_x, couples].astype(F32)
        gain_inv[core, k] = 1.0 / jnp.sum(tile[:PARTS], axis=0, keepdims=True)
    push_gain = pltpu.make_async_remote_copy(
        src_ref=gain_inv.at[core],
        dst_ref=gain_inv.at[core],
        send_sem=gain_send,
        recv_sem=gain_recv,
        device_id=(a, sibling),
        device_id_type=MESH,
    )
    push_gain.start()

    for i in range(n_attn):
        b = wrap(a + i, n_attn)
        for other in range(CORES):
            def arrived(b=b, other=other):
                pltpu.make_async_copy(
                    part_recv.at[b, other],
                    part_recv.at[b, other],
                    rs_recv.at[b * CORES + other],
                ).wait()

            if i > 0:
                arrived()
            else:
                pl.when(core != other)(arrived)

    load_res.wait()
    totals = []
    for other in range(CORES):
        total = part_recv[0, other].astype(F32)
        for b in range(1, n_attn):
            total = total + part_recv[b, other].astype(F32)
        totals.append(total)
    state = res_buf[...] + jnp.concatenate(
        [totals[other][xx * req : (xx + 1) * req] for xx in range(n_x) for other in range(CORES)],
        axis=0,
    )
    out[...] = state
    scaled = (state * gain_buf[...]).astype(BF16)

    def push_x(zz, to_a, to_lane):
        return pltpu.make_async_remote_copy(
            src_ref=x_send.at[(zz * n_attn + to_a) * per_z + to_lane],
            dst_ref=x_recv.at[e, a],
            send_sem=xs_sem,
            recv_sem=xr_sem.at[z],
            device_id=(to_a, zz * per_z + to_lane),
            device_id_type=MESH,
        )

    around = [*range(1, n_attn), 0]
    for dz in far:
        zz = wrap(z + dz, n_z)
        picked = dot(select[zz], scaled).astype(BF16)
        x_send[pl.ds(zz * n_exp, n_exp)] = picked.reshape(n_exp, CAP, HD)

        def start_x(k, carry, zz=zz, dz=dz):
            to = wrap(lane + per_z // 2 + k, per_z)
            for i in around:
                copy = push_x(zz, wrap(a + i, n_attn), to)
                if dz == 0 and i == 0:
                    pl.when(to != lane)(copy.start)
                else:
                    copy.start()
            return carry

        lax.fori_loop(0, per_z, start_x, 0)
    own_x = pltpu.make_async_copy(
        x_send.at[(z * n_attn + a) * per_z + lane], x_recv.at[e, a], xr_sem.at[z]
    )
    own_x.start()

    squares = jnp.zeros((rows, HD), F32)
    push_gain.wait_recv()
    for step, dz in enumerate(far):
        zz = wrap(z + n_z - dz, n_z)
        arrived = x_recv.at[pl.ds(zz * per_z, per_z)]
        pltpu.make_async_copy(arrived, arrived, xr_sem.at[zz]).wait()
        load_gate_up(zz).wait()
        pieces = [x_recv[zz * per_z + q].reshape(rows, HD) for q in range(per_z)]
        for q in range(per_z):
            plain = pieces[q].astype(F32) * gain_inv[q % CORES, zz * n_x + q // CORES]
            squares = squares + plain * plain
        left = jnp.concatenate(pieces, axis=1)
        product = dot(left, gate_up_buf[pl.ds(pl.multiple_of(zz * depth, depth), depth), :])
        if step == 0:
            mixed[...] = product
        else:
            mixed[...] += product

    scale = lax.rsqrt(jnp.sum(squares, axis=1, keepdims=True) / features + 1e-06)
    gate = mixed[:, :width] * scale
    up = mixed[:, width:] * scale
    inner = (gate / (1.0 + jnp.exp(-gate)) * up).astype(BF16)

    load_down.wait()

    def push_y(to_a, to_e):
        return pltpu.make_async_remote_copy(
            src_ref=y_send.at[to_e * n_attn + to_a],
            dst_ref=y_recv.at[(z * n_attn + a) * per_z + lane],
            send_sem=ys_sem,
            recv_sem=yr_sem.at[z],
            device_id=(to_a, to_e),
            device_id_type=MESH,
        )

    for dz in far:
        zz = wrap(z + dz, n_z)
        produced = dot(
            inner, down_buf[:, pl.ds(pl.multiple_of(zz * depth, depth), depth)]
        ).astype(BF16)
        for q in range(per_z):
            y_send[pl.ds((zz * per_z + q) * n_attn, n_attn)] = produced[
                :, q * HD : (q + 1) * HD
            ].reshape(n_attn, CAP, HD)

        def start_y(k, carry, zz=zz, dz=dz):
            to = wrap(lane + per_z // 2 + k, per_z)
            for i in around:
                copy = push_y(wrap(a + i, n_attn), zz * per_z + to)
                if dz == 0 and i == 0:
                    pl.when(to != lane)(copy.start)
                else:
                    copy.start()
            return carry

        lax.fori_loop(0, per_z, start_y, 0)
    own_y = pltpu.make_async_copy(
        y_send.at[e * n_attn + a], y_recv.at[(z * n_attn + a) * per_z + lane], yr_sem.at[z]
    )
    own_y.start()

    for dz in far:
        p = wrap(z + n_z - dz, n_z)
        arrived = y_recv.at[pl.ds(p * n_exp, n_exp)]
        pltpu.make_async_copy(arrived, arrived, yr_sem.at[p]).wait()
        back = y_recv[pl.ds(p * n_exp, n_exp)].reshape(slots, HD)
        out[...] += dot(comb_high[p], back) + dot(comb_low[p], back)

    for copy in sent:
        copy.wait_send()
    for q in range(2):
        push_w(q).wait_send()
    push_gain.wait_send()
    for b in range(n_attn):
        for other in range(CORES):
            def left_here(b=b, other=other):
                push_part(b, other).wait_send()

            pl.when(jnp.logical_not((b == a) & (core == other)))(left_here)
    for buffer, sem in ((x_send, xs_sem), (y_send, ys_sem)):
        gone = buffer.at[pl.ds(0, experts - 1)]
        pltpu.make_async_copy(gone, gone, sem).wait()


def body(
    n_attn,
    n_exp,
    residual,
    queries,
    keys,
    values,
    lengths,
    out_weight,
    norm_gain,
    expert_ids,
    gates,
    gate_up,
    down,
):
    req, span = keys.shape[0], keys.shape[1]
    heads = queries.shape[1] // HD
    width = down.shape[1]
    features = gate_up.shape[1]
    block = residual.shape[0]
    n_z = n_attn
    n_x = n_exp // (CORES * n_z)
    rows = n_attn * CAP
    slots = n_exp * CAP
    half = n_x * req
    groups = 4
    top = expert_ids.shape[1]
    cfg = (n_attn, n_z, n_x, req, heads, width)
    anywhere = pl.BlockSpec(memory_space=pl.ANY)
    vmem = pltpu.VMEM
    sem = pltpu.SemaphoreType.DMA
    return pl.pallas_call(
        functools.partial(layer_kernel, cfg),
        out_shape=jax.ShapeDtypeStruct(residual.shape, F32),
        in_specs=[anywhere] * 11,
        out_specs=pl.BlockSpec(memory_space=pltpu.VMEM),
        scratch_shapes=[
            vmem(queries.shape, BF16),
            vmem((req * heads, HD), BF16),
            vmem((req * heads, HD), BF16),
            vmem(keys.shape, BF16),
            vmem(values.shape, BF16),
            vmem((2, CORES, heads // 2, HD, HD), BF16),
            vmem(residual.shape, F32),
            pltpu.SMEM(lengths.shape, jnp.int32),
            vmem((1, HD), F32),
            vmem((CORES, n_z * n_x, 1, HD), F32),
            vmem((top, block), jnp.int32),
            vmem((top, block), F32),
            vmem((2, n_z, n_x, heads // 2 + 1, req, HD), BF16),
            vmem((n_attn, CORES, half, HD), BF16),
            vmem((n_attn, CORES, half, HD), BF16),
            vmem((n_attn, slots, block), BF16),
            vmem((n_attn, block, slots), BF16),
            vmem((n_attn, block, slots), BF16),
            vmem((n_attn * n_exp, CAP, HD), BF16),
            vmem((n_exp, n_attn, CAP, HD), BF16),
            vmem((features, 2 * width), BF16),
            vmem((width, features), BF16),
            vmem((rows, 2 * width), F32),
            vmem((n_exp * n_attn, CAP, HD), BF16),
            vmem((n_attn * n_exp, CAP, HD), BF16),
            sem((9,)),
            sem((groups,)),
            sem((groups,)),
            sem((n_z,)),
            sem((2,)),
            sem((2,)),
            sem,
            sem,
            sem((2, 2, max(n_x, n_z) - 1)),
            sem((2, max(n_x, n_z) - 1, max(n_x, n_z) - 1)),
            sem((2, n_z, n_x)),
            sem((n_attn * CORES,)),
            sem((n_attn * CORES,)),
            sem,
            sem((n_z,)),
            sem,
            sem((n_attn,)),
        ],
        compiler_params=pltpu.CompilerParams(
            collective_id=0, has_side_effects=True, vmem_limit_bytes=58 * 1024 * 1024
        ),
        name="layer",
    )(
        lengths,
        residual,
        queries,
        keys,
        values,
        out_weight.reshape(heads // 2, 2, HD, HD),
        norm_gain.reshape(1, HD),
        expert_ids.T,
        gates.T,
        gate_up,
        down,
    )


def solution(mesh):
    in_specs = (
        P("attn", "expert"),
        P("expert", "attn"),
        P("expert", None, "attn"),
        P("expert", None, "attn"),
        P("expert"),
        P("attn", "expert"),
        P("expert"),
        P("attn", None),
        P("attn", None),
        P(("attn", "expert"), None, None),
        P(("attn", "expert"), None, None),
    )
    run = functools.partial(body, mesh.shape["attn"], mesh.shape["expert"])
    return jax.shard_map(
        run, mesh=mesh, in_specs=in_specs, out_specs=P("attn", "expert"), check_vma=False
    )
```

```python
import functools
import math

import jax
import jax.numpy as jnp
from jax import lax
from jax.experimental import pallas as pl
from jax.experimental.pallas import tpu as pltpu
from jax.sharding import PartitionSpec as P

HD = 128
CAP = 16
CORES = 2
PARTS = 3
F32 = jnp.float32
BF16 = jnp.bfloat16
MESH = pl.DeviceIdType.MESH
NT = (((1,), (1,)), ((), ()))


def dot(left, right):
    return jnp.dot(left, right, preferred_element_type=F32)


def dot_nt(left, right):
    return lax.dot_general(left, right, NT, preferred_element_type=F32)


def layer_kernel(
    cfg,
    lengths,
    residual,
    queries,
    keys,
    values,
    out_weight,
    gain,
    ids,
    gates,
    gate_up,
    down,
    out,
    q_in,
    q_rows,
    o_rows,
    k_buf,
    v_buf,
    w_buf,
    res_buf,
    len_buf,
    gain_buf,
    gain_inv,
    ids_buf,
    gates_buf,
    att,
    part_send,
    part_recv,
    select,
    comb_high,
    comb_low,
    x_send,
    x_recv,
    gate_up_buf,
    down_buf,
    mixed,
    y_send,
    y_recv,
    in_sem,
    k_sem,
    v_sem,
    gate_sem,
    w_send,
    w_recv,
    gain_send,
    gain_recv,
    own_send,
    pass_send,
    att_recv,
    rs_send,
    rs_recv,
    xs_sem,
    xr_sem,
    ys_sem,
    yr_sem,
):
    n_attn, n_z, n_x, req, heads, width = cfg
    n_exp = n_z * n_x * CORES
    per_z = n_x * CORES
    block = per_z * req
    half = n_x * req
    features = n_exp * HD
    slots = n_exp * CAP
    experts = n_attn * n_exp
    part_req = req // 2
    couples = heads // 2
    places = n_attn // 2
    far = [n_z // 2, *(d for d in range(1, n_z) if d != n_z // 2), 0]
    a = lax.axis_index("attn")
    e = lax.axis_index("expert")
    core = lax.rem(e, CORES)
    chip = lax.div(e, CORES)
    x = lax.rem(chip, n_x)
    z = lax.div(chip, n_x)
    sibling = chip * CORES + (1 - core)
    lane = lax.rem(e, per_z)

    def wrap(value, size):
        return lax.rem(value, size)

    def ring(size):
        return sorted(range(1, size), key=lambda d: min(d, size - d))

    n_group = k_sem.shape[0]
    group = req // n_group
    load_q = pltpu.make_async_copy(queries, q_in, in_sem.at[8])
    load_len = pltpu.make_async_copy(lengths, len_buf, in_sem.at[6])
    load_q.start()
    load_len.start()

    def load_k(g):
        span = pl.ds(g * group, group)
        return pltpu.make_async_copy(keys.at[span], k_buf.at[span], k_sem.at[g])

    def load_v(g):
        span = pl.ds(g * group, group)
        return pltpu.make_async_copy(values.at[span], v_buf.at[span], v_sem.at[g])

    for g in range(n_group):
        load_k(g).start()
        load_v(g).start()

    def load_w(q):
        return pltpu.make_async_copy(out_weight.at[:, q], w_buf.at[q, core], in_sem.at[q])

    load_gain = pltpu.make_async_copy(gain, gain_buf, in_sem.at[7])
    load_res = pltpu.make_async_copy(residual, res_buf, in_sem.at[2])
    load_ids = pltpu.make_async_copy(ids, ids_buf, in_sem.at[3])
    load_gates = pltpu.make_async_copy(gates, gates_buf, in_sem.at[4])
    for load in (load_gain, load_res, load_ids, load_gates, load_w(0), load_w(1)):
        load.start()

    barrier = pltpu.get_barrier_semaphore()
    known = [(a, (z * n_x + wrap(x + d, n_x)) * CORES + core) for d in range(1, n_x)]
    known += [(a, (wrap(z + d, n_z) * n_x + x) * CORES + core) for d in range(1, n_z)]
    known += [(a, sibling)]
    known += [
        (wrap(a + i, n_attn), chip * CORES + other)
        for i in range(1, n_attn)
        for other in range(CORES)
    ]
    for device in known:
        pl.semaphore_signal(barrier, inc=1, device_id=device, device_id_type=MESH)

    load_q.wait()
    load_len.wait()
    pairs = (heads * req, heads * req)
    first = lax.broadcasted_iota(jnp.int32, pairs, 0)
    second = lax.broadcasted_iota(jnp.int32, pairs, 1)
    by_request = (lax.div(first, heads) == lax.rem(second, req)) & (
        lax.rem(first, heads) == lax.div(second, req)
    )
    stacked = jnp.concatenate([q_in[:, h * HD : (h + 1) * HD] for h in range(heads)], axis=0)
    q_rows[...] = dot(by_request.astype(F32).astype(BF16), stacked).astype(BF16)
    span = k_buf.shape[1]
    position = lax.broadcasted_iota(jnp.int32, (heads, span), 1)

    def score(g):
        load_k(g).wait()
        return [
            dot_nt(q_rows[i * heads : (i + 1) * heads, :], k_buf[i])
            for i in range(g * group, (g + 1) * group)
        ]

    def quarter(part, side, item_z, item_x):
        count = couples // 2
        extra = 1 if part == 0 and side == 1 else 0
        return att.at[part, item_z, item_x, pl.ds(side * count, count + extra)]

    def along(axis, part, side, item_z, item_x, d, sem):
        item = quarter(part, side, item_z, item_x)
        if axis == 0:
            to = z * n_x + wrap(x + d, n_x)
        else:
            to = wrap(z + d, n_z) * n_x + x
        return pltpu.make_async_remote_copy(
            src_ref=item,
            dst_ref=item,
            send_sem=sem,
            recv_sem=att_recv.at[part, side, item_z, item_x],
            device_id=(a, to * CORES + core),
            device_id_type=MESH,
        )

    def att_arrived(part, side, item_z, item_x):
        item = quarter(part, side, item_z, item_x)
        pltpu.make_async_copy(item, item, att_recv.at[part, side, item_z, item_x]).wait()

    rings = (ring(n_x), ring(n_z))

    def own_away(part, second):
        for k in range(max(n_x, n_z) - 1):
            for side in range(2):
                axis = 1 - side if second else side
                if k < len(rings[axis]):
                    copy = along(
                        axis, part, side, z, x, rings[axis][k], own_send.at[part, side, axis, k]
                    )
                    copy.start()
                    sent.append(copy)

    def pass_on(part):
        for k in range(max(n_x, n_z) - 1):
            for side in range(2):
                if k < len(rings[side]):
                    d = rings[side][k]
                    from_z = wrap(z + d, n_z) if side else z
                    from_x = x if side else wrap(x + d, n_x)
                    att_arrived(part, side, from_z, from_x)
                    for m, onward in enumerate(rings[1 - side]):
                        copy = along(
                            1 - side, part, side, from_z, from_x, onward, pass_send.at[part, side, k, m]
                        )
                        copy.start()
                        sent.append(copy)

    sent = []
    mesh_pairs = (heads * part_req, heads * part_req)
    to_row = lax.broadcasted_iota(jnp.int32, mesh_pairs, 0)
    from_row = lax.broadcasted_iota(jnp.int32, mesh_pairs, 1)
    by_head = (
        (lax.div(from_row, heads) == lax.rem(to_row, part_req))
        & (lax.rem(from_row, heads) == lax.div(to_row, part_req))
    ).astype(F32).astype(BF16)

    def leave(part):
        span = heads * part_req
        own = dot(by_head, o_rows[part * span : (part + 1) * span, :]).astype(BF16)
        att[part, z, x, :couples] = own.reshape(couples, 2 * part_req, HD)
        if part == 0:
            load_gain.wait()
            place = lax.broadcasted_iota(jnp.int32, (2 * part_req, HD), 0)
            rest = gain_buf[...]
            tile = jnp.zeros((2 * part_req, HD), F32)
            for k in range(PARTS):
                piece = rest.astype(BF16).astype(F32)
                tile = tile + jnp.where(place == k, piece, 0.0)
                rest = rest - piece
            att[0, z, x, couples] = tile.astype(BF16)
            pl.semaphore_wait(barrier, len(known))
        own_away(part, False)
        if part == 1:
            pass_on(0)
        own_away(part, True)

    ahead = score(0)
    for g in range(n_group):
        scores = ahead
        if g + 1 < n_group:
            ahead = score(g + 1)
        weights = []
        for j in range(group):
            masked = jnp.where(
                position < len_buf[g * group + j], scores[j] * (1.0 / math.sqrt(HD)), -1e30
            )
            expo = jnp.exp(masked - jnp.max(masked, axis=1, keepdims=True))
            weights.append((expo / jnp.sum(expo, axis=1, keepdims=True)).astype(BF16))
        load_v(g).wait()
        results = [dot(weights[j], v_buf[g * group + j]).astype(BF16) for j in range(group)]
        o_rows[g * group * heads : (g + 1) * group * heads, :] = jnp.concatenate(results, axis=0)
        if (g + 1) % (n_group // 2) == 0:
            leave(2 * g // n_group)

    def push_w(q):
        return pltpu.make_async_remote_copy(
            src_ref=out_weight.at[:, q],
            dst_ref=w_buf.at[q, core],
            send_sem=w_send.at[q],
            recv_sem=w_recv.at[q],
            device_id=(a, sibling),
            device_id_type=MESH,
        )

    for q in range(2):
        push_w(q).start()

    pass_on(1)

    depth = per_z * HD

    def load_gate_up(g):
        part = pl.ds(pl.multiple_of(g * depth, depth), depth)
        return pltpu.make_async_copy(
            gate_up.at[0, part, :], gate_up_buf.at[part, :], gate_sem.at[g]
        )

    load_down = pltpu.make_async_copy(down.at[0], down_buf, in_sem.at[5])
    for g in range(n_z):
        load_gate_up(g).start()
    load_down.start()

    load_ids.wait()
    load_gates.wait()
    earlier = (
        lax.broadcasted_iota(jnp.int32, (block, block), 0)
        < lax.broadcasted_iota(jnp.int32, (block, block), 1)
    ).astype(F32).astype(BF16)
    spread_row = lax.broadcasted_iota(jnp.int32, (slots, n_exp), 0)
    spread_col = lax.broadcasted_iota(jnp.int32, (slots, n_exp), 1)
    spread = (
        ((spread_row >= spread_col * CAP) & (spread_row < (spread_col + 1) * CAP))
        .astype(F32)
        .astype(BF16)
    )
    slot = lax.rem(lax.broadcasted_iota(jnp.int32, (slots, block), 0), CAP).astype(F32)
    local = lax.broadcasted_iota(jnp.int32, (n_exp, block), 0)
    turn = lax.div(local, per_z)
    turn = lax.div(turn, places) + 2 * lax.rem(turn, places)
    first_named = lax.rem(a + turn, n_attn) * n_exp + lax.rem(local, per_z)
    for p in range(n_z):
        named = first_named + p * per_z
        chosen = jnp.zeros((n_exp, block), F32)
        weight = jnp.zeros((n_exp, block), F32)
        for k in range(ids_buf.shape[0]):
            hit = ids_buf[k : k + 1, :] == named
            chosen = chosen + jnp.where(hit, 1.0, 0.0)
            weight = weight + jnp.where(hit, gates_buf[k : k + 1, :], 0.0)
        rank = dot(chosen.astype(BF16), earlier)
        high = weight.astype(BF16)
        low = (weight - high.astype(F32)).astype(BF16)
        table = jnp.concatenate([rank.astype(BF16), chosen.astype(BF16), high, low], axis=1)
        wide = dot(spread, table)
        here = wide[:, :block] == slot
        select[p] = jnp.where(here, wide[:, block : 2 * block], 0.0).astype(BF16)
        comb_high[p] = jnp.where(here, wide[:, 2 * block : 3 * block], 0.0).T.astype(BF16)
        comb_low[p] = jnp.where(here, wide[:, 3 * block :], 0.0).T.astype(BF16)

    for q in range(2):
        load_w(q).wait()
        push_w(q).wait_recv()
    right = jnp.concatenate(
        [
            w_buf[q, other].reshape(couples * HD, HD)
            for q in range(2)
            for other in range(CORES)
        ],
        axis=1,
    )

    def push_part(b, other):
        return pltpu.make_async_remote_copy(
            src_ref=part_send.at[b, other],
            dst_ref=part_recv.at[a, core],
            send_sem=rs_send.at[b * CORES + other],
            recv_sem=rs_recv.at[a * CORES + core],
            device_id=(b, chip * CORES + other),
            device_id_type=MESH,
        )

    for i in [0, *ring(n_z)]:
        b = wrap(z + i, n_z)
        for part in range(2):
            for d in ring(n_x):
                att_arrived(part, 1, b, wrap(x + d, n_x))
            if i > 0:
                for d in [0, *ring(n_x)]:
                    att_arrived(part, 0, b, wrap(x + d, n_x))
        left = jnp.concatenate(
            [att[:, b, :, k].reshape(2 * half, HD) for k in range(couples)], axis=1
        )
        wide = dot(left, right)
        pieces = []
        for xx in range(n_x):
            for part in range(2):
                top = (part * n_x + xx) * 2 * part_req
                pieces.append(
                    wide[top : top + part_req, : CORES * HD]
                    + wide[top + part_req : top + 2 * part_req, CORES * HD :]
                )
        product = jnp.concatenate(pieces, axis=0)
        for other in range(CORES):
            part_send[b, other] = product[:, other * HD : (other + 1) * HD].astype(BF16)

        @pl.when(b != a)
        def _():
            for other in range(CORES):
                push_part(b, other).start()

        @pl.when(b == a)
        def _():
            push_part(b, 1 - core).start()
            part_recv[a, core] = part_send[b, core]

    for k in range(n_z * n_x):
        tile = att[0, k // n_x, k % n_x, couples].astype(F32)
        gain_inv[core, k] = 1.0 / jnp.sum(tile[:PARTS], axis=0, keepdims=True)
    push_gain = pltpu.make_async_remote_copy(
        src_ref=gain_inv.at[core],
        dst_ref=gain_inv.at[core],
        send_sem=gain_send,
        recv_sem=gain_recv,
        device_id=(a, sibling),
        device_id_type=MESH,
    )
    push_gain.start()

    for i in range(n_attn):
        b = wrap(a + i, n_attn)
        for other in range(CORES):
            def arrived(b=b, other=other):
                pltpu.make_async_copy(
                    part_recv.at[b, other],
                    part_recv.at[b, other],
                    rs_recv.at[b * CORES + other],
                ).wait()

            if i > 0:
                arrived()
            else:
                pl.when(core != other)(arrived)

    load_res.wait()
    totals = []
    for other in range(CORES):
        total = part_recv[0, other].astype(F32)
        for b in range(1, n_attn):
            total = total + part_recv[b, other].astype(F32)
        totals.append(total)
    state = res_buf[...] + jnp.concatenate(
        [totals[other][xx * req : (xx + 1) * req] for xx in range(n_x) for other in range(CORES)],
        axis=0,
    )
    out[...] = state
    scaled = (state * gain_buf[...]).astype(BF16)

    def spot(zz, even, place, to_lane):
        return ((zz * 2 + even) * places + place) * per_z + to_lane

    def back_place(even, place):
        return (n_attn - even - 2 * place) % n_attn // 2

    def push_x(even, place, zz, to_lane):
        return pltpu.make_async_remote_copy(
            src_ref=x_send.at[spot(zz, even, place, to_lane)],
            dst_ref=x_recv.at[even, e, back_place(even, place)],
            send_sem=xs_sem,
            recv_sem=xr_sem.at[even, z],
            device_id=(wrap(a + even + 2 * place, n_attn), zz * per_z + to_lane),
            device_id_type=MESH,
        )

    def spread_out(push, even, dz):
        zz = wrap(z + dz, n_z)

        def step(k, carry):
            to = wrap(lane + per_z // 2 + k, per_z)
            for place in reversed(range(places)):
                copy = push(even, place, zz, to)
                if dz == 0 and even == 0 and place == 0:
                    pl.when(to != lane)(copy.start)
                else:
                    copy.start()
            return carry

        lax.fori_loop(0, per_z, step, 0)

    for dz in far:
        zz = wrap(z + dz, n_z)
        picked = dot(select[zz], scaled).astype(BF16)
        x_send[pl.ds(zz * n_exp, n_exp)] = picked.reshape(n_exp, CAP, HD)
        spread_out(push_x, 0, dz)
    own_x = pltpu.make_async_copy(
        x_send.at[spot(z, 0, 0, lane)], x_recv.at[0, e, 0], xr_sem.at[0, z]
    )
    own_x.start()
    for dz in far:
        spread_out(push_x, 1, dz)

    def push_y(even, place, zz, to_lane):
        return pltpu.make_async_remote_copy(
            src_ref=y_send.at[zz * per_z + to_lane, even, place],
            dst_ref=y_recv.at[even, z, back_place(even, place), lane],
            send_sem=ys_sem,
            recv_sem=yr_sem.at[even, z],
            device_id=(wrap(a + even + 2 * place, n_attn), zz * per_z + to_lane),
            device_id_type=MESH,
        )

    push_gain.wait_recv()
    part_rows = places * CAP
    for even in range(2):
        squares = jnp.zeros((part_rows, HD), F32)
        for step, dz in enumerate(far):
            zz = wrap(z + n_z - dz, n_z)
            arrived = x_recv.at[even, pl.ds(zz * per_z, per_z)]
            pltpu.make_async_copy(arrived, arrived, xr_sem.at[even, zz]).wait()
            if even == 0:
                load_gate_up(zz).wait()
            pieces = [x_recv[even, zz * per_z + q].reshape(part_rows, HD) for q in range(per_z)]
            for q in range(per_z):
                plain = pieces[q].astype(F32) * gain_inv[q % CORES, zz * n_x + q // CORES]
                squares = squares + plain * plain
            left = jnp.concatenate(pieces, axis=1)
            product = dot(left, gate_up_buf[pl.ds(pl.multiple_of(zz * depth, depth), depth), :])
            if step == 0:
                mixed[...] = product
            else:
                mixed[...] += product
        scale = lax.rsqrt(jnp.sum(squares, axis=1, keepdims=True) / features + 1e-06)
        gate = mixed[:, :width] * scale
        up = mixed[:, width:] * scale
        inner = (gate / (1.0 + jnp.exp(-gate)) * up).astype(BF16)

        if even == 0:
            load_down.wait()
        for dz in far:
            zz = wrap(z + dz, n_z)
            produced = dot(
                inner, down_buf[:, pl.ds(pl.multiple_of(zz * depth, depth), depth)]
            ).astype(BF16)
            for q in range(per_z):
                y_send[zz * per_z + q, even] = produced[:, q * HD : (q + 1) * HD].reshape(
                    places, CAP, HD
                )
            spread_out(push_y, even, dz)
        if even == 0:
            own_y = pltpu.make_async_copy(
                y_send.at[e, 0, 0], y_recv.at[0, z, 0, lane], yr_sem.at[0, z]
            )
            own_y.start()

    part_slots = slots // 2
    for even in range(2):
        for dz in far:
            zz = wrap(z + n_z - dz, n_z)
            arrived = y_recv.at[even, zz]
            pltpu.make_async_copy(arrived, arrived, yr_sem.at[even, zz]).wait()
            back = y_recv[even, zz].reshape(part_slots, HD)
            lanes = slice(even * part_slots, (even + 1) * part_slots)
            out[...] += dot(comb_high[zz, :, lanes], back) + dot(comb_low[zz, :, lanes], back)

    for copy in sent:
        copy.wait_send()
    for q in range(2):
        push_w(q).wait_send()
    push_gain.wait_send()
    for b in range(n_attn):
        for other in range(CORES):
            def left_here(b=b, other=other):
                push_part(b, other).wait_send()

            pl.when(jnp.logical_not((b == a) & (core == other)))(left_here)
    for sem in (xs_sem, ys_sem):
        gone = x_send.at[pl.ds(0, experts - 1)]
        pltpu.make_async_copy(gone, gone, sem).wait()


def body(
    n_attn,
    n_exp,
    residual,
    queries,
    keys,
    values,
    lengths,
    out_weight,
    norm_gain,
    expert_ids,
    gates,
    gate_up,
    down,
):
    req, span = keys.shape[0], keys.shape[1]
    heads = queries.shape[1] // HD
    width = down.shape[1]
    features = gate_up.shape[1]
    block = residual.shape[0]
    n_z = n_attn
    n_x = n_exp // (CORES * n_z)
    rows = n_attn * CAP
    slots = n_exp * CAP
    half = n_x * req
    groups = 4
    top = expert_ids.shape[1]
    cfg = (n_attn, n_z, n_x, req, heads, width)
    anywhere = pl.BlockSpec(memory_space=pl.ANY)
    vmem = pltpu.VMEM
    sem = pltpu.SemaphoreType.DMA
    return pl.pallas_call(
        functools.partial(layer_kernel, cfg),
        out_shape=pltpu.VMEM(residual.shape, F32),
        in_specs=[anywhere] * 11,
        out_specs=pl.BlockSpec(memory_space=pltpu.VMEM),
        scratch_shapes=[
            vmem(queries.shape, BF16),
            vmem((req * heads, HD), BF16),
            vmem((req * heads, HD), BF16),
            vmem(keys.shape, BF16),
            vmem(values.shape, BF16),
            vmem((2, CORES, heads // 2, HD, HD), BF16),
            vmem(residual.shape, F32),
            pltpu.SMEM(lengths.shape, jnp.int32),
            vmem((1, HD), F32),
            vmem((CORES, n_z * n_x, 1, HD), F32),
            vmem((top, block), jnp.int32),
            vmem((top, block), F32),
            vmem((2, n_z, n_x, heads // 2 + 1, req, HD), BF16),
            vmem((n_attn, CORES, half, HD), BF16),
            vmem((n_attn, CORES, half, HD), BF16),
            vmem((n_attn, slots, block), BF16),
            vmem((n_attn, block, slots), BF16),
            vmem((n_attn, block, slots), BF16),
            vmem((n_attn * n_exp, CAP, HD), BF16),
            vmem((2, n_exp, n_attn // 2, CAP, HD), BF16),
            vmem((features, 2 * width), BF16),
            vmem((width, features), BF16),
            vmem((rows // 2, 2 * width), F32),
            vmem((n_exp, 2, n_attn // 2, CAP, HD), BF16),
            vmem((2, n_z, n_attn // 2, n_x * CORES, CAP, HD), BF16),
            sem((9,)),
            sem((groups,)),
            sem((groups,)),
            sem((n_z,)),
            sem((2,)),
            sem((2,)),
            sem,
            sem,
            sem((2, 2, 2, max(n_x, n_z) - 1)),
            sem((2, 2, max(n_x, n_z) - 1, max(n_x, n_z) - 1)),
            sem((2, 2, n_z, n_x)),
            sem((n_attn * CORES,)),
            sem((n_attn * CORES,)),
            sem,
            sem((2, n_z)),
            sem,
            sem((2, n_z)),
        ],
        compiler_params=pltpu.CompilerParams(
            collective_id=0, has_side_effects=True, vmem_limit_bytes=58 * 1024 * 1024
        ),
        name="layer",
    )(
        lengths,
        residual,
        queries,
        keys,
        values,
        out_weight.reshape(heads // 2, 2, HD, HD),
        norm_gain.reshape(1, HD),
        expert_ids.T,
        gates.T,
        gate_up,
        down,
    )


def solution(mesh):
    in_specs = (
        P("attn", "expert"),
        P("expert", "attn"),
        P("expert", None, "attn"),
        P("expert", None, "attn"),
        P("expert"),
        P("attn", "expert"),
        P("expert"),
        P("attn", None),
        P("attn", None),
        P(("attn", "expert"), None, None),
        P(("attn", "expert"), None, None),
    )
    run = functools.partial(body, mesh.shape["attn"], mesh.shape["expert"])
    return jax.shard_map(
        run, mesh=mesh, in_specs=in_specs, out_specs=P("attn", "expert"), check_vma=False
    )
```

```python
import functools
import math

import jax
import jax.numpy as jnp
from jax import lax
from jax.experimental import pallas as pl
from jax.experimental.pallas import tpu as pltpu
from jax.sharding import PartitionSpec as P

HD = 128
CAP = 16
CORES = 2
PARTS = 3
F32 = jnp.float32
BF16 = jnp.bfloat16
MESH = pl.DeviceIdType.MESH
NT = (((1,), (1,)), ((), ()))


def dot(left, right):
    return jnp.dot(left, right, preferred_element_type=F32)


def dot_nt(left, right):
    return lax.dot_general(left, right, NT, preferred_element_type=F32)


def layer_kernel(
    cfg,
    lengths,
    residual,
    queries,
    keys,
    values,
    out_weight,
    gain,
    ids,
    gates,
    gate_up,
    down,
    out,
    q_in,
    q_rows,
    o_rows,
    k_buf,
    v_buf,
    w_buf,
    res_buf,
    len_buf,
    gain_buf,
    gain_inv,
    ids_buf,
    gates_buf,
    att,
    part_send,
    part_recv,
    select,
    comb_high,
    comb_low,
    x_send,
    x_recv,
    gate_up_buf,
    down_buf,
    mixed,
    y_send,
    y_recv,
    in_sem,
    k_sem,
    v_sem,
    gate_sem,
    w_send,
    w_recv,
    gain_send,
    gain_recv,
    own_send,
    pass_send,
    att_recv,
    rs_send,
    rs_recv,
    xs_sem,
    xr_sem,
    ys_sem,
    yr_sem,
):
    n_attn, n_z, n_x, req, heads, width = cfg
    n_exp = n_z * n_x * CORES
    per_z = n_x * CORES
    block = per_z * req
    half = n_x * req
    features = n_exp * HD
    slots = n_exp * CAP
    rows = n_attn * CAP
    experts = n_attn * n_exp
    part_req = req // 2
    couples = heads // 2
    far = [n_z // 2, *(d for d in range(1, n_z) if d != n_z // 2), 0]
    a = lax.axis_index("attn")
    e = lax.axis_index("expert")
    core = lax.rem(e, CORES)
    chip = lax.div(e, CORES)
    x = lax.rem(chip, n_x)
    z = lax.div(chip, n_x)
    sibling = chip * CORES + (1 - core)
    lane = lax.rem(e, per_z)

    def wrap(value, size):
        return lax.rem(value, size)

    def ring(size):
        return sorted(range(1, size), key=lambda d: min(d, size - d))

    n_group = k_sem.shape[0]
    group = req // n_group
    load_q = pltpu.make_async_copy(queries, q_in, in_sem.at[8])
    load_len = pltpu.make_async_copy(lengths, len_buf, in_sem.at[6])
    load_q.start()
    load_len.start()

    def load_k(g):
        span = pl.ds(g * group, group)
        return pltpu.make_async_copy(keys.at[span], k_buf.at[span], k_sem.at[g])

    def load_v(g):
        span = pl.ds(g * group, group)
        return pltpu.make_async_copy(values.at[span], v_buf.at[span], v_sem.at[g])

    for g in range(n_group):
        load_k(g).start()
        load_v(g).start()

    def load_w(q):
        return pltpu.make_async_copy(out_weight.at[:, q], w_buf.at[q, core], in_sem.at[q])

    load_gain = pltpu.make_async_copy(gain, gain_buf, in_sem.at[7])
    load_res = pltpu.make_async_copy(residual, res_buf, in_sem.at[2])
    load_ids = pltpu.make_async_copy(ids, ids_buf, in_sem.at[3])
    load_gates = pltpu.make_async_copy(gates, gates_buf, in_sem.at[4])
    for load in (load_gain, load_res, load_ids, load_gates, load_w(0), load_w(1)):
        load.start()

    barrier = pltpu.get_barrier_semaphore()
    known = [(a, (z * n_x + wrap(x + d, n_x)) * CORES + core) for d in range(1, n_x)]
    known += [(a, (wrap(z + d, n_z) * n_x + x) * CORES + core) for d in range(1, n_z)]
    known += [(a, sibling)]
    known += [
        (wrap(a + i, n_attn), chip * CORES + other)
        for i in range(1, n_attn)
        for other in range(CORES)
    ]
    for device in known:
        pl.semaphore_signal(barrier, inc=1, device_id=device, device_id_type=MESH)

    load_q.wait()
    load_len.wait()
    pairs = (heads * req, heads * req)
    first = lax.broadcasted_iota(jnp.int32, pairs, 0)
    second = lax.broadcasted_iota(jnp.int32, pairs, 1)
    by_request = (lax.div(first, heads) == lax.rem(second, req)) & (
        lax.rem(first, heads) == lax.div(second, req)
    )
    stacked = jnp.concatenate([q_in[:, h * HD : (h + 1) * HD] for h in range(heads)], axis=0)
    q_rows[...] = dot(by_request.astype(F32).astype(BF16), stacked).astype(BF16)
    span = k_buf.shape[1]
    position = lax.broadcasted_iota(jnp.int32, (heads, span), 1)

    def score(g):
        load_k(g).wait()
        return [
            dot_nt(q_rows[i * heads : (i + 1) * heads, :], k_buf[i])
            for i in range(g * group, (g + 1) * group)
        ]

    def quarter(part, side, item_z, item_x):
        count = couples // 2
        extra = 1 if part == 0 and side == 1 else 0
        return att.at[part, item_z, item_x, pl.ds(side * count, count + extra)]

    def along(axis, part, side, item_z, item_x, d, sem):
        item = quarter(part, side, item_z, item_x)
        if axis == 0:
            to = z * n_x + wrap(x + d, n_x)
        else:
            to = wrap(z + d, n_z) * n_x + x
        return pltpu.make_async_remote_copy(
            src_ref=item,
            dst_ref=item,
            send_sem=sem,
            recv_sem=att_recv.at[part, side, item_z, item_x],
            device_id=(a, to * CORES + core),
            device_id_type=MESH,
        )

    def att_arrived(part, side, item_z, item_x):
        item = quarter(part, side, item_z, item_x)
        pltpu.make_async_copy(item, item, att_recv.at[part, side, item_z, item_x]).wait()

    rings = (ring(n_x), ring(n_z))

    def own_away(part, second):
        for k in range(max(n_x, n_z) - 1):
            for side in range(2):
                axis = 1 - side if second else side
                if k < len(rings[axis]):
                    copy = along(
                        axis, part, side, z, x, rings[axis][k], own_send.at[part, side, axis, k]
                    )
                    copy.start()
                    sent.append(copy)

    def pass_on(part):
        for k in range(max(n_x, n_z) - 1):
            for side in range(2):
                if k < len(rings[side]):
                    d = rings[side][k]
                    from_z = wrap(z + d, n_z) if side else z
                    from_x = x if side else wrap(x + d, n_x)
                    att_arrived(part, side, from_z, from_x)
                    for m, onward in enumerate(rings[1 - side]):
                        copy = along(
                            1 - side, part, side, from_z, from_x, onward, pass_send.at[part, side, k, m]
                        )
                        copy.start()
                        sent.append(copy)

    sent = []
    mesh_pairs = (heads * part_req, heads * part_req)
    to_row = lax.broadcasted_iota(jnp.int32, mesh_pairs, 0)
    from_row = lax.broadcasted_iota(jnp.int32, mesh_pairs, 1)
    by_head = (
        (lax.div(from_row, heads) == lax.rem(to_row, part_req))
        & (lax.rem(from_row, heads) == lax.div(to_row, part_req))
    ).astype(F32).astype(BF16)

    def leave(part):
        span = heads * part_req
        own = dot(by_head, o_rows[part * span : (part + 1) * span, :]).astype(BF16)
        att[part, z, x, :couples] = own.reshape(couples, 2 * part_req, HD)
        if part == 0:
            load_gain.wait()
            place = lax.broadcasted_iota(jnp.int32, (2 * part_req, HD), 0)
            rest = gain_buf[...]
            tile = jnp.zeros((2 * part_req, HD), F32)
            for k in range(PARTS):
                piece = rest.astype(BF16).astype(F32)
                tile = tile + jnp.where(place == k, piece, 0.0)
                rest = rest - piece
            att[0, z, x, couples] = tile.astype(BF16)
            pl.semaphore_wait(barrier, len(known))
        own_away(part, False)
        if part == 1:
            pass_on(0)
        own_away(part, True)

    ahead = score(0)
    for g in range(n_group):
        scores = ahead
        if g + 1 < n_group:
            ahead = score(g + 1)
        weights = []
        for j in range(group):
            masked = jnp.where(
                position < len_buf[g * group + j], scores[j] * (1.0 / math.sqrt(HD)), -1e30
            )
            expo = jnp.exp(masked - jnp.max(masked, axis=1, keepdims=True))
            weights.append((expo / jnp.sum(expo, axis=1, keepdims=True)).astype(BF16))
        load_v(g).wait()
        results = [dot(weights[j], v_buf[g * group + j]).astype(BF16) for j in range(group)]
        o_rows[g * group * heads : (g + 1) * group * heads, :] = jnp.concatenate(results, axis=0)
        if (g + 1) % (n_group // 2) == 0:
            leave(2 * g // n_group)

    def push_w(q):
        return pltpu.make_async_remote_copy(
            src_ref=out_weight.at[:, q],
            dst_ref=w_buf.at[q, core],
            send_sem=w_send.at[q],
            recv_sem=w_recv.at[q],
            device_id=(a, sibling),
            device_id_type=MESH,
        )

    for q in range(2):
        push_w(q).start()

    pass_on(1)

    depth = per_z * HD

    def load_gate_up(g):
        part = pl.ds(pl.multiple_of(g * depth, depth), depth)
        return pltpu.make_async_copy(
            gate_up.at[0, part, :], gate_up_buf.at[part, :], gate_sem.at[g]
        )

    load_down = pltpu.make_async_copy(down.at[0], down_buf, in_sem.at[5])
    for g in range(n_z):
        load_gate_up(g).start()
    load_down.start()

    load_ids.wait()
    load_gates.wait()
    earlier = (
        lax.broadcasted_iota(jnp.int32, (block, block), 0)
        < lax.broadcasted_iota(jnp.int32, (block, block), 1)
    ).astype(F32).astype(BF16)
    spread_row = lax.broadcasted_iota(jnp.int32, (slots, n_exp), 0)
    spread_col = lax.broadcasted_iota(jnp.int32, (slots, n_exp), 1)
    spread = (
        ((spread_row >= spread_col * CAP) & (spread_row < (spread_col + 1) * CAP))
        .astype(F32)
        .astype(BF16)
    )
    slot = lax.rem(lax.broadcasted_iota(jnp.int32, (slots, block), 0), CAP).astype(F32)
    local = lax.broadcasted_iota(jnp.int32, (n_exp, block), 0)
    for p in range(n_z):
        named = lax.div(local, per_z) * n_exp + p * per_z + lax.rem(local, per_z)
        chosen = jnp.zeros((n_exp, block), F32)
        weight = jnp.zeros((n_exp, block), F32)
        for k in range(ids_buf.shape[0]):
            hit = ids_buf[k : k + 1, :] == named
            chosen = chosen + jnp.where(hit, 1.0, 0.0)
            weight = weight + jnp.where(hit, gates_buf[k : k + 1, :], 0.0)
        rank = dot(chosen.astype(BF16), earlier)
        high = weight.astype(BF16)
        low = (weight - high.astype(F32)).astype(BF16)
        table = jnp.concatenate([rank.astype(BF16), chosen.astype(BF16), high, low], axis=1)
        wide = dot(spread, table)
        here = wide[:, :block] == slot
        select[p] = jnp.where(here, wide[:, block : 2 * block], 0.0).astype(BF16)
        comb_high[p] = jnp.where(here, wide[:, 2 * block : 3 * block], 0.0).T.astype(BF16)
        comb_low[p] = jnp.where(here, wide[:, 3 * block :], 0.0).T.astype(BF16)

    for q in range(2):
        load_w(q).wait()
        push_w(q).wait_recv()
    right = jnp.concatenate(
        [
            w_buf[q, other].reshape(couples * HD, HD)
            for q in range(2)
            for other in range(CORES)
        ],
        axis=1,
    )

    def push_part(b, other):
        return pltpu.make_async_remote_copy(
            src_ref=part_send.at[b, other],
            dst_ref=part_recv.at[a, core],
            send_sem=rs_send.at[b * CORES + other],
            recv_sem=rs_recv.at[a * CORES + core],
            device_id=(b, chip * CORES + other),
            device_id_type=MESH,
        )

    for i in [0, *ring(n_z)]:
        b = wrap(z + i, n_z)
        for part in range(2):
            for d in ring(n_x):
                att_arrived(part, 1, b, wrap(x + d, n_x))
            if i > 0:
                for d in [0, *ring(n_x)]:
                    att_arrived(part, 0, b, wrap(x + d, n_x))
        left = jnp.concatenate(
            [att[:, b, :, k].reshape(2 * half, HD) for k in range(couples)], axis=1
        )
        wide = dot(left, right)
        pieces = []
        for xx in range(n_x):
            for part in range(2):
                top = (part * n_x + xx) * 2 * part_req
                pieces.append(
                    wide[top : top + part_req, : CORES * HD]
                    + wide[top + part_req : top + 2 * part_req, CORES * HD :]
                )
        product = jnp.concatenate(pieces, axis=0)
        for other in range(CORES):
            part_send[b, other] = product[:, other * HD : (other + 1) * HD].astype(BF16)

        @pl.when(b != a)
        def _():
            for other in range(CORES):
                push_part(b, other).start()

        @pl.when(b == a)
        def _():
            push_part(b, 1 - core).start()
            part_recv[a, core] = part_send[b, core]

    for k in range(n_z * n_x):
        tile = att[0, k // n_x, k % n_x, couples].astype(F32)
        gain_inv[core, k] = 1.0 / jnp.sum(tile[:PARTS], axis=0, keepdims=True)
    push_gain = pltpu.make_async_remote_copy(
        src_ref=gain_inv.at[core],
        dst_ref=gain_inv.at[core],
        send_sem=gain_send,
        recv_sem=gain_recv,
        device_id=(a, sibling),
        device_id_type=MESH,
    )
    push_gain.start()

    for i in range(n_attn):
        b = wrap(a + i, n_attn)
        for other in range(CORES):
            def arrived(b=b, other=other):
                pltpu.make_async_copy(
                    part_recv.at[b, other],
                    part_recv.at[b, other],
                    rs_recv.at[b * CORES + other],
                ).wait()

            if i > 0:
                arrived()
            else:
                pl.when(core != other)(arrived)

    load_res.wait()
    totals = []
    for other in range(CORES):
        total = part_recv[0, other].astype(F32)
        for b in range(1, n_attn):
            total = total + part_recv[b, other].astype(F32)
        totals.append(total)
    state = res_buf[...] + jnp.concatenate(
        [totals[other][xx * req : (xx + 1) * req] for xx in range(n_x) for other in range(CORES)],
        axis=0,
    )
    out[...] = state
    scaled = (state * gain_buf[...]).astype(BF16)

    def push_x(zz, to_a, to_lane):
        return pltpu.make_async_remote_copy(
            src_ref=x_send.at[(zz * n_attn + to_a) * per_z + to_lane],
            dst_ref=x_recv.at[e, a],
            send_sem=xs_sem,
            recv_sem=xr_sem.at[z],
            device_id=(to_a, zz * per_z + to_lane),
            device_id_type=MESH,
        )

    around = [*range(1, n_attn), 0]
    for dz in far:
        zz = wrap(z + dz, n_z)
        picked = dot(select[zz], scaled).astype(BF16)
        x_send[pl.ds(zz * n_exp, n_exp)] = picked.reshape(n_exp, CAP, HD)

        def start_x(k, carry, zz=zz, dz=dz):
            to = wrap(lane + per_z // 2 + k, per_z)
            for i in around:
                copy = push_x(zz, wrap(a + i, n_attn), to)
                if dz == 0 and i == 0:
                    pl.when(to != lane)(copy.start)
                else:
                    copy.start()
            return carry

        lax.fori_loop(0, per_z, start_x, 0)
    own_x = pltpu.make_async_copy(
        x_send.at[(z * n_attn + a) * per_z + lane], x_recv.at[e, a], xr_sem.at[z]
    )
    own_x.start()

    for copy in sent:
        copy.wait_send()
    for q in range(2):
        push_w(q).wait_send()
    push_gain.wait_send()
    for b in range(n_attn):
        for other in range(CORES):
            def left_here(b=b, other=other):
                push_part(b, other).wait_send()

            pl.when(jnp.logical_not((b == a) & (core == other)))(left_here)

    squares = jnp.zeros((rows, HD), F32)
    push_gain.wait_recv()
    for step, dz in enumerate(far):
        zz = wrap(z + n_z - dz, n_z)
        arrived = x_recv.at[pl.ds(zz * per_z, per_z)]
        pltpu.make_async_copy(arrived, arrived, xr_sem.at[zz]).wait()
        load_gate_up(zz).wait()
        pieces = [x_recv[zz * per_z + q].reshape(rows, HD) for q in range(per_z)]
        for q in range(per_z):
            plain = pieces[q].astype(F32) * gain_inv[q % CORES, zz * n_x + q // CORES]
            squares = squares + plain * plain
        left = jnp.concatenate(pieces, axis=1)
        product = dot(left, gate_up_buf[pl.ds(pl.multiple_of(zz * depth, depth), depth), :])
        if step == 0:
            mixed[...] = product
        else:
            mixed[...] += product

    scale = lax.rsqrt(jnp.sum(squares, axis=1, keepdims=True) / features + 1e-06)
    gate = mixed[:, :width] * scale
    up = mixed[:, width:] * scale
    inner = (gate / (1.0 + jnp.exp(-gate)) * up).astype(BF16)

    load_down.wait()

    def push_y(to_a, to_e):
        return pltpu.make_async_remote_copy(
            src_ref=y_send.at[to_e * n_attn + to_a],
            dst_ref=y_recv.at[(z * n_attn + a) * per_z + lane],
            send_sem=ys_sem,
            recv_sem=yr_sem.at[z],
            device_id=(to_a, to_e),
            device_id_type=MESH,
        )

    for dz in far:
        zz = wrap(z + dz, n_z)
        produced = dot(
            inner, down_buf[:, pl.ds(pl.multiple_of(zz * depth, depth), depth)]
        ).astype(BF16)
        for q in range(per_z):
            y_send[pl.ds((zz * per_z + q) * n_attn, n_attn)] = produced[
                :, q * HD : (q + 1) * HD
            ].reshape(n_attn, CAP, HD)

        def start_y(k, carry, zz=zz, dz=dz):
            to = wrap(lane + per_z // 2 + k, per_z)
            for i in around:
                copy = push_y(wrap(a + i, n_attn), zz * per_z + to)
                if dz == 0 and i == 0:
                    pl.when(to != lane)(copy.start)
                else:
                    copy.start()
            return carry

        lax.fori_loop(0, per_z, start_y, 0)
    own_y = pltpu.make_async_copy(
        y_send.at[e * n_attn + a], y_recv.at[(z * n_attn + a) * per_z + lane], yr_sem.at[z]
    )
    own_y.start()

    for dz in far:
        p = wrap(z + n_z - dz, n_z)
        arrived = y_recv.at[pl.ds(p * n_exp, n_exp)]
        pltpu.make_async_copy(arrived, arrived, yr_sem.at[p]).wait()
        back = y_recv[pl.ds(p * n_exp, n_exp)].reshape(slots, HD)
        out[...] += dot(comb_high[p], back) + dot(comb_low[p], back)

    for buffer, sem in ((x_send, xs_sem), (y_send, ys_sem)):
        gone = buffer.at[pl.ds(0, experts - 1)]
        pltpu.make_async_copy(gone, gone, sem).wait()


def body(
    n_attn,
    n_exp,
    residual,
    queries,
    keys,
    values,
    lengths,
    out_weight,
    norm_gain,
    expert_ids,
    gates,
    gate_up,
    down,
):
    req, span = keys.shape[0], keys.shape[1]
    heads = queries.shape[1] // HD
    width = down.shape[1]
    features = gate_up.shape[1]
    block = residual.shape[0]
    n_z = n_attn
    n_x = n_exp // (CORES * n_z)
    rows = n_attn * CAP
    slots = n_exp * CAP
    half = n_x * req
    groups = 4
    top = expert_ids.shape[1]
    cfg = (n_attn, n_z, n_x, req, heads, width)
    anywhere = pl.BlockSpec(memory_space=pl.ANY)
    vmem = pltpu.VMEM
    sem = pltpu.SemaphoreType.DMA
    return pl.pallas_call(
        functools.partial(layer_kernel, cfg),
        out_shape=pltpu.VMEM(residual.shape, F32),
        in_specs=[anywhere] * 11,
        out_specs=pl.BlockSpec(memory_space=pltpu.VMEM),
        scratch_shapes=[
            vmem(queries.shape, BF16),
            vmem((req * heads, HD), BF16),
            vmem((req * heads, HD), BF16),
            vmem(keys.shape, BF16),
            vmem(values.shape, BF16),
            vmem((2, CORES, heads // 2, HD, HD), BF16),
            vmem(residual.shape, F32),
            pltpu.SMEM(lengths.shape, jnp.int32),
            vmem((1, HD), F32),
            vmem((CORES, n_z * n_x, 1, HD), F32),
            vmem((top, block), jnp.int32),
            vmem((top, block), F32),
            vmem((2, n_z, n_x, heads // 2 + 1, req, HD), BF16),
            vmem((n_attn, CORES, half, HD), BF16),
            vmem((n_attn, CORES, half, HD), BF16),
            vmem((n_attn, slots, block), BF16),
            vmem((n_attn, block, slots), BF16),
            vmem((n_attn, block, slots), BF16),
            vmem((n_attn * n_exp, CAP, HD), BF16),
            vmem((n_exp, n_attn, CAP, HD), BF16),
            vmem((features, 2 * width), BF16),
            vmem((width, features), BF16),
            vmem((rows, 2 * width), F32),
            vmem((n_exp * n_attn, CAP, HD), BF16),
            vmem((n_attn * n_exp, CAP, HD), BF16),
            sem((9,)),
            sem((groups,)),
            sem((groups,)),
            sem((n_z,)),
            sem((2,)),
            sem((2,)),
            sem,
            sem,
            sem((2, 2, 2, max(n_x, n_z) - 1)),
            sem((2, 2, max(n_x, n_z) - 1, max(n_x, n_z) - 1)),
            sem((2, 2, n_z, n_x)),
            sem((n_attn * CORES,)),
            sem((n_attn * CORES,)),
            sem,
            sem((n_z,)),
            sem,
            sem((n_attn,)),
        ],
        compiler_params=pltpu.CompilerParams(
            collective_id=0, has_side_effects=True, vmem_limit_bytes=58 * 1024 * 1024
        ),
        name="layer",
    )(
        lengths,
        residual,
        queries,
        keys,
        values,
        out_weight.reshape(heads // 2, 2, HD, HD),
        norm_gain.reshape(1, HD),
        expert_ids.T,
        gates.T,
        gate_up,
        down,
    )


def solution(mesh):
    in_specs = (
        P("attn", "expert"),
        P("expert", "attn"),
        P("expert", None, "attn"),
        P("expert", None, "attn"),
        P("expert"),
        P("attn", "expert"),
        P("expert"),
        P("attn", None),
        P("attn", None),
        P(("attn", "expert"), None, None),
        P(("attn", "expert"), None, None),
    )
    run = functools.partial(body, mesh.shape["attn"], mesh.shape["expert"])
    return jax.shard_map(
        run, mesh=mesh, in_specs=in_specs, out_specs=P("attn", "expert"), check_vma=False
    )
```

```python
import functools
import math

import jax
import jax.numpy as jnp
from jax import lax
from jax.experimental import pallas as pl
from jax.experimental.pallas import tpu as pltpu
from jax.sharding import PartitionSpec as P

HD = 128
CAP = 16
CORES = 2
PARTS = 3
F32 = jnp.float32
BF16 = jnp.bfloat16
MESH = pl.DeviceIdType.MESH
NT = (((1,), (1,)), ((), ()))


def dot(left, right):
    return jnp.dot(left, right, preferred_element_type=F32)


def dot_nt(left, right):
    return lax.dot_general(left, right, NT, preferred_element_type=F32)


def layer_kernel(
    cfg,
    lengths,
    residual,
    queries,
    keys,
    values,
    out_weight,
    gain,
    ids,
    gates,
    gate_up,
    down,
    out,
    q_in,
    q_rows,
    o_rows,
    k_buf,
    v_buf,
    w_buf,
    res_buf,
    len_buf,
    gain_buf,
    gain_inv,
    ids_buf,
    gates_buf,
    att,
    part_send,
    part_recv,
    select,
    comb,
    x_send,
    x_recv,
    gate_up_buf,
    down_buf,
    mixed,
    y_send,
    y_recv,
    in_sem,
    k_sem,
    v_sem,
    gate_sem,
    w_send,
    w_recv,
    gain_send,
    gain_recv,
    own_send,
    pass_send,
    att_recv,
    rs_send,
    rs_recv,
    xs_sem,
    xr_sem,
    ys_sem,
    yr_sem,
):
    n_attn, n_z, n_x, req, heads, width = cfg
    n_exp = n_z * n_x * CORES
    per_z = n_x * CORES
    block = per_z * req
    half = n_x * req
    features = n_exp * HD
    slots = n_exp * CAP
    rows = n_attn * CAP
    experts = n_attn * n_exp
    part_req = req // 2
    couples = heads // 2
    far = [n_z // 2, *(d for d in range(1, n_z) if d != n_z // 2), 0]
    a = lax.axis_index("attn")
    e = lax.axis_index("expert")
    core = lax.rem(e, CORES)
    chip = lax.div(e, CORES)
    x = lax.rem(chip, n_x)
    z = lax.div(chip, n_x)
    sibling = chip * CORES + (1 - core)
    lane = lax.rem(e, per_z)

    def wrap(value, size):
        return lax.rem(value, size)

    def ring(size):
        return sorted(range(1, size), key=lambda d: min(d, size - d))

    n_group = k_sem.shape[0]
    group = req // n_group
    load_q = pltpu.make_async_copy(queries, q_in, in_sem.at[8])
    load_len = pltpu.make_async_copy(lengths, len_buf, in_sem.at[6])
    load_q.start()
    load_len.start()

    def load_k(g):
        span = pl.ds(g * group, group)
        return pltpu.make_async_copy(keys.at[span], k_buf.at[span], k_sem.at[g])

    def load_v(g):
        span = pl.ds(g * group, group)
        return pltpu.make_async_copy(values.at[span], v_buf.at[span], v_sem.at[g])

    for g in range(n_group):
        load_k(g).start()
        load_v(g).start()

    def load_w(q):
        return pltpu.make_async_copy(out_weight.at[:, q], w_buf.at[q, core], in_sem.at[q])

    load_gain = pltpu.make_async_copy(gain, gain_buf, in_sem.at[7])
    load_res = pltpu.make_async_copy(residual, res_buf, in_sem.at[2])
    load_ids = pltpu.make_async_copy(ids, ids_buf, in_sem.at[3])
    load_gates = pltpu.make_async_copy(gates, gates_buf, in_sem.at[4])
    for load in (load_gain, load_res, load_ids, load_gates, load_w(0), load_w(1)):
        load.start()

    barrier = pltpu.get_barrier_semaphore()
    known = [(a, (z * n_x + wrap(x + d, n_x)) * CORES + core) for d in range(1, n_x)]
    known += [(a, (wrap(z + d, n_z) * n_x + x) * CORES + core) for d in range(1, n_z)]
    known += [(a, sibling)]
    known += [
        (wrap(a + i, n_attn), chip * CORES + other)
        for i in range(1, n_attn)
        for other in range(CORES)
    ]
    for device in known:
        pl.semaphore_signal(barrier, inc=1, device_id=device, device_id_type=MESH)

    load_q.wait()
    load_len.wait()
    pairs = (heads * req, heads * req)
    first = lax.broadcasted_iota(jnp.int32, pairs, 0)
    second = lax.broadcasted_iota(jnp.int32, pairs, 1)
    by_request = (lax.div(first, heads) == lax.rem(second, req)) & (
        lax.rem(first, heads) == lax.div(second, req)
    )
    stacked = jnp.concatenate([q_in[:, h * HD : (h + 1) * HD] for h in range(heads)], axis=0)
    q_rows[...] = dot(by_request.astype(F32).astype(BF16), stacked).astype(BF16)
    span = k_buf.shape[1]
    position = lax.broadcasted_iota(jnp.int32, (heads, span), 1)

    def score(g):
        load_k(g).wait()
        return [
            dot_nt(q_rows[i * heads : (i + 1) * heads, :], k_buf[i])
            for i in range(g * group, (g + 1) * group)
        ]

    def quarter(part, side, item_z, item_x):
        count = couples // 2
        extra = 1 if part == 0 and side == 1 else 0
        return att.at[part, item_z, item_x, pl.ds(side * count, count + extra)]

    def along(axis, part, side, item_z, item_x, d, sem):
        item = quarter(part, side, item_z, item_x)
        if axis == 0:
            to = z * n_x + wrap(x + d, n_x)
        else:
            to = wrap(z + d, n_z) * n_x + x
        return pltpu.make_async_remote_copy(
            src_ref=item,
            dst_ref=item,
            send_sem=sem,
            recv_sem=att_recv.at[part, side, item_z, item_x],
            device_id=(a, to * CORES + core),
            device_id_type=MESH,
        )

    def att_arrived(part, side, item_z, item_x):
        item = quarter(part, side, item_z, item_x)
        pltpu.make_async_copy(item, item, att_recv.at[part, side, item_z, item_x]).wait()

    rings = (ring(n_x), ring(n_z))

    def own_away(part, second):
        for k in range(max(n_x, n_z) - 1):
            for side in range(2):
                axis = 1 - side if second else side
                if k < len(rings[axis]):
                    copy = along(
                        axis, part, side, z, x, rings[axis][k], own_send.at[part, side, axis, k]
                    )
                    copy.start()
                    sent.append(copy)

    def pass_on(part):
        for k in range(max(n_x, n_z) - 1):
            for side in range(2):
                if k < len(rings[side]):
                    d = rings[side][k]
                    from_z = wrap(z + d, n_z) if side else z
                    from_x = x if side else wrap(x + d, n_x)
                    att_arrived(part, side, from_z, from_x)
                    for m, onward in enumerate(rings[1 - side]):
                        copy = along(
                            1 - side, part, side, from_z, from_x, onward, pass_send.at[part, side, k, m]
                        )
                        copy.start()
                        sent.append(copy)

    sent = []
    mesh_pairs = (heads * part_req, heads * part_req)
    to_row = lax.broadcasted_iota(jnp.int32, mesh_pairs, 0)
    from_row = lax.broadcasted_iota(jnp.int32, mesh_pairs, 1)
    by_head = (
        (lax.div(from_row, heads) == lax.rem(to_row, part_req))
        & (lax.rem(from_row, heads) == lax.div(to_row, part_req))
    ).astype(F32).astype(BF16)

    def leave(part):
        span = heads * part_req
        own = dot(by_head, o_rows[part * span : (part + 1) * span, :]).astype(BF16)
        att[part, z, x, :couples] = own.reshape(couples, 2 * part_req, HD)
        if part == 0:
            load_gain.wait()
            place = lax.broadcasted_iota(jnp.int32, (2 * part_req, HD), 0)
            rest = gain_buf[...]
            tile = jnp.zeros((2 * part_req, HD), F32)
            for k in range(PARTS):
                piece = rest.astype(BF16).astype(F32)
                tile = tile + jnp.where(place == k, piece, 0.0)
                rest = rest - piece
            att[0, z, x, couples] = tile.astype(BF16)
            pl.semaphore_wait(barrier, len(known))
        own_away(part, False)
        if part == 1:
            own_away(0, True)
            pass_on(0)
            own_away(1, True)

    ahead = score(0)
    for g in range(n_group):
        scores = ahead
        if g + 1 < n_group:
            ahead = score(g + 1)
        weights = []
        for j in range(group):
            masked = jnp.where(
                position < len_buf[g * group + j], scores[j] * (1.0 / math.sqrt(HD)), -1e30
            )
            expo = jnp.exp(masked - jnp.max(masked, axis=1, keepdims=True))
            weights.append((expo / jnp.sum(expo, axis=1, keepdims=True)).astype(BF16))
        load_v(g).wait()
        results = [dot(weights[j], v_buf[g * group + j]).astype(BF16) for j in range(group)]
        o_rows[g * group * heads : (g + 1) * group * heads, :] = jnp.concatenate(results, axis=0)
        if (g + 1) % (n_group // 2) == 0:
            leave(2 * g // n_group)

    def push_w(q):
        return pltpu.make_async_remote_copy(
            src_ref=out_weight.at[:, q],
            dst_ref=w_buf.at[q, core],
            send_sem=w_send.at[q],
            recv_sem=w_recv.at[q],
            device_id=(a, sibling),
            device_id_type=MESH,
        )

    for q in range(2):
        push_w(q).start()

    pass_on(1)

    depth = per_z * HD

    def load_gate_up(g):
        part = pl.ds(pl.multiple_of(g * depth, depth), depth)
        return pltpu.make_async_copy(
            gate_up.at[0, part, :], gate_up_buf.at[part, :], gate_sem.at[g]
        )

    load_down = pltpu.make_async_copy(down.at[0], down_buf, in_sem.at[5])
    for g in range(n_z):
        load_gate_up(g).start()
    load_down.start()

    load_ids.wait()
    load_gates.wait()
    earlier = (
        lax.broadcasted_iota(jnp.int32, (block, block), 0)
        < lax.broadcasted_iota(jnp.int32, (block, block), 1)
    ).astype(F32).astype(BF16)
    spread_row = lax.broadcasted_iota(jnp.int32, (slots, n_exp), 0)
    spread_col = lax.broadcasted_iota(jnp.int32, (slots, n_exp), 1)
    spread = (
        ((spread_row >= spread_col * CAP) & (spread_row < (spread_col + 1) * CAP))
        .astype(F32)
        .astype(BF16)
    )
    slot = lax.rem(lax.broadcasted_iota(jnp.int32, (slots, block), 0), CAP).astype(F32)
    local = lax.broadcasted_iota(jnp.int32, (n_exp, block), 0)
    for p in range(n_z):
        named = lax.div(local, per_z) * n_exp + p * per_z + lax.rem(local, per_z)
        chosen = jnp.zeros((n_exp, block), F32)
        weight = jnp.zeros((n_exp, block), F32)
        for k in range(ids_buf.shape[0]):
            hit = ids_buf[k : k + 1, :] == named
            chosen = chosen + jnp.where(hit, 1.0, 0.0)
            weight = weight + jnp.where(hit, gates_buf[k : k + 1, :], 0.0)
        rank = dot(chosen.astype(BF16), earlier)
        high = weight.astype(BF16)
        low = (weight - high.astype(F32)).astype(BF16)
        table = jnp.concatenate([rank.astype(BF16), chosen.astype(BF16), high, low], axis=1)
        wide = dot(spread, table)
        here = wide[:, :block] == slot
        select[p] = jnp.where(here, wide[:, block : 2 * block], 0.0).astype(BF16)
        comb[p, :block] = jnp.where(here, wide[:, 2 * block : 3 * block], 0.0).T.astype(BF16)
        comb[p, block:] = jnp.where(here, wide[:, 3 * block :], 0.0).T.astype(BF16)

    for q in range(2):
        load_w(q).wait()
        push_w(q).wait_recv()
    right = jnp.concatenate(
        [
            w_buf[q, other].reshape(couples * HD, HD)
            for q in range(2)
            for other in range(CORES)
        ],
        axis=1,
    )

    def push_part(b, other):
        return pltpu.make_async_remote_copy(
            src_ref=part_send.at[b, other],
            dst_ref=part_recv.at[a, core],
            send_sem=rs_send.at[b * CORES + other],
            recv_sem=rs_recv.at[a * CORES + core],
            device_id=(b, chip * CORES + other),
            device_id_type=MESH,
        )

    for i in [0, *ring(n_z)]:
        b = wrap(z + i, n_z)
        for part in range(2):
            for d in ring(n_x):
                att_arrived(part, 1, b, wrap(x + d, n_x))
            if i > 0:
                for d in [0, *ring(n_x)]:
                    att_arrived(part, 0, b, wrap(x + d, n_x))
        left = jnp.concatenate(
            [att[:, b, :, k].reshape(2 * half, HD) for k in range(couples)], axis=1
        )
        wide = dot(left, right)
        pieces = []
        for xx in range(n_x):
            for part in range(2):
                top = (part * n_x + xx) * 2 * part_req
                pieces.append(
                    wide[top : top + part_req, : CORES * HD]
                    + wide[top + part_req : top + 2 * part_req, CORES * HD :]
                )
        product = jnp.concatenate(pieces, axis=0)
        for other in range(CORES):
            part_send[b, other] = product[:, other * HD : (other + 1) * HD].astype(BF16)

        @pl.when(b != a)
        def _():
            for other in range(CORES):
                push_part(b, other).start()

        @pl.when(b == a)
        def _():
            push_part(b, 1 - core).start()
            part_recv[a, core] = part_send[b, core]

    for k in range(n_z * n_x):
        tile = att[0, k // n_x, k % n_x, couples].astype(F32)
        gain_inv[core, k] = 1.0 / jnp.sum(tile[:PARTS], axis=0, keepdims=True)
    push_gain = pltpu.make_async_remote_copy(
        src_ref=gain_inv.at[core],
        dst_ref=gain_inv.at[core],
        send_sem=gain_send,
        recv_sem=gain_recv,
        device_id=(a, sibling),
        device_id_type=MESH,
    )
    push_gain.start()

    for i in range(n_attn):
        b = wrap(a + i, n_attn)
        for other in range(CORES):
            def arrived(b=b, other=other):
                pltpu.make_async_copy(
                    part_recv.at[b, other],
                    part_recv.at[b, other],
                    rs_recv.at[b * CORES + other],
                ).wait()

            if i > 0:
                arrived()
            else:
                pl.when(core != other)(arrived)

    load_res.wait()
    totals = []
    for other in range(CORES):
        total = part_recv[0, other].astype(F32)
        for b in range(1, n_attn):
            total = total + part_recv[b, other].astype(F32)
        totals.append(total)
    state = res_buf[...] + jnp.concatenate(
        [totals[other][xx * req : (xx + 1) * req] for xx in range(n_x) for other in range(CORES)],
        axis=0,
    )
    out[...] = state
    scaled = (state * gain_buf[...]).astype(BF16)

    def push_x(zz, to_a, to_lane):
        return pltpu.make_async_remote_copy(
            src_ref=x_send.at[(zz * n_attn + to_a) * per_z + to_lane],
            dst_ref=x_recv.at[e, a],
            send_sem=xs_sem,
            recv_sem=xr_sem.at[z],
            device_id=(to_a, zz * per_z + to_lane),
            device_id_type=MESH,
        )

    around = [*range(1, n_attn), 0]
    for dz in far:
        zz = wrap(z + dz, n_z)
        picked = dot(select[zz], scaled).astype(BF16)
        x_send[pl.ds(zz * n_exp, n_exp)] = picked.reshape(n_exp, CAP, HD)

        def start_x(k, carry, zz=zz, dz=dz):
            to = wrap(lane + per_z // 2 + k, per_z)
            for i in around:
                copy = push_x(zz, wrap(a + i, n_attn), to)
                if dz == 0 and i == 0:
                    pl.when(to != lane)(copy.start)
                else:
                    copy.start()
            return carry

        lax.fori_loop(0, per_z, start_x, 0)
    own_x = pltpu.make_async_copy(
        x_send.at[(z * n_attn + a) * per_z + lane], x_recv.at[e, a], xr_sem.at[z]
    )
    own_x.start()

    for copy in sent:
        copy.wait_send()
    for q in range(2):
        push_w(q).wait_send()
    push_gain.wait_send()
    for b in range(n_attn):
        for other in range(CORES):
            def left_here(b=b, other=other):
                push_part(b, other).wait_send()

            pl.when(jnp.logical_not((b == a) & (core == other)))(left_here)

    squares = jnp.zeros((rows, HD), F32)
    push_gain.wait_recv()
    for step, dz in enumerate(far):
        zz = wrap(z + n_z - dz, n_z)
        arrived = x_recv.at[pl.ds(zz * per_z, per_z)]
        pltpu.make_async_copy(arrived, arrived, xr_sem.at[zz]).wait()
        load_gate_up(zz).wait()
        pieces = [x_recv[zz * per_z + q].reshape(rows, HD) for q in range(per_z)]
        for q in range(per_z):
            plain = pieces[q].astype(F32) * gain_inv[q % CORES, zz * n_x + q // CORES]
            squares = squares + plain * plain
        left = jnp.concatenate(pieces, axis=1)
        product = dot(left, gate_up_buf[pl.ds(pl.multiple_of(zz * depth, depth), depth), :])
        if step == 0:
            mixed[...] = product
        else:
            mixed[...] += product

    scale = lax.rsqrt(jnp.sum(squares, axis=1, keepdims=True) / features + 1e-06)
    gate = mixed[:, :width] * scale
    up = mixed[:, width:] * scale
    inner = (gate / (1.0 + jnp.exp(-gate)) * up).astype(BF16)

    load_down.wait()

    def push_y(to_a, to_e):
        return pltpu.make_async_remote_copy(
            src_ref=y_send.at[to_e * n_attn + to_a],
            dst_ref=y_recv.at[(z * n_attn + a) * per_z + lane],
            send_sem=ys_sem,
            recv_sem=yr_sem.at[z],
            device_id=(to_a, to_e),
            device_id_type=MESH,
        )

    for dz in far:
        zz = wrap(z + dz, n_z)
        produced = dot(
            inner, down_buf[:, pl.ds(pl.multiple_of(zz * depth, depth), depth)]
        ).astype(BF16)
        for q in range(per_z):
            y_send[pl.ds((zz * per_z + q) * n_attn, n_attn)] = produced[
                :, q * HD : (q + 1) * HD
            ].reshape(n_attn, CAP, HD)

        def start_y(k, carry, zz=zz, dz=dz):
            to = wrap(lane + per_z // 2 + k, per_z)
            for i in around:
                copy = push_y(wrap(a + i, n_attn), zz * per_z + to)
                if dz == 0 and i == 0:
                    pl.when(to != lane)(copy.start)
                else:
                    copy.start()
            return carry

        lax.fori_loop(0, per_z, start_y, 0)
    own_y = pltpu.make_async_copy(
        y_send.at[e * n_attn + a], y_recv.at[(z * n_attn + a) * per_z + lane], yr_sem.at[z]
    )
    own_y.start()

    for dz in far:
        p = wrap(z + n_z - dz, n_z)
        arrived = y_recv.at[pl.ds(p * n_exp, n_exp)]
        pltpu.make_async_copy(arrived, arrived, yr_sem.at[p]).wait()
        back = y_recv[pl.ds(p * n_exp, n_exp)].reshape(slots, HD)
        both = dot(comb[p], back)
        out[...] += both[:block] + both[block:]

    for buffer, sem in ((x_send, xs_sem), (y_send, ys_sem)):
        gone = buffer.at[pl.ds(0, experts - 1)]
        pltpu.make_async_copy(gone, gone, sem).wait()


def body(
    n_attn,
    n_exp,
    residual,
    queries,
    keys,
    values,
    lengths,
    out_weight,
    norm_gain,
    expert_ids,
    gates,
    gate_up,
    down,
):
    req, span = keys.shape[0], keys.shape[1]
    heads = queries.shape[1] // HD
    width = down.shape[1]
    features = gate_up.shape[1]
    block = residual.shape[0]
    n_z = n_attn
    n_x = n_exp // (CORES * n_z)
    rows = n_attn * CAP
    slots = n_exp * CAP
    half = n_x * req
    groups = 4
    top = expert_ids.shape[1]
    cfg = (n_attn, n_z, n_x, req, heads, width)
    anywhere = pl.BlockSpec(memory_space=pl.ANY)
    vmem = pltpu.VMEM
    sem = pltpu.SemaphoreType.DMA
    return pl.pallas_call(
        functools.partial(layer_kernel, cfg),
        out_shape=pltpu.VMEM(residual.shape, F32),
        in_specs=[anywhere] * 11,
        out_specs=pl.BlockSpec(memory_space=pltpu.VMEM),
        scratch_shapes=[
            vmem(queries.shape, BF16),
            vmem((req * heads, HD), BF16),
            vmem((req * heads, HD), BF16),
            vmem(keys.shape, BF16),
            vmem(values.shape, BF16),
            vmem((2, CORES, heads // 2, HD, HD), BF16),
            vmem(residual.shape, F32),
            pltpu.SMEM(lengths.shape, jnp.int32),
            vmem((1, HD), F32),
            vmem((CORES, n_z * n_x, 1, HD), F32),
            vmem((top, block), jnp.int32),
            vmem((top, block), F32),
            vmem((2, n_z, n_x, heads // 2 + 1, req, HD), BF16),
            vmem((n_attn, CORES, half, HD), BF16),
            vmem((n_attn, CORES, half, HD), BF16),
            vmem((n_attn, slots, block), BF16),
            vmem((n_z, 2 * block, slots), BF16),
            vmem((n_attn * n_exp, CAP, HD), BF16),
            vmem((n_exp, n_attn, CAP, HD), BF16),
            vmem((features, 2 * width), BF16),
            vmem((width, features), BF16),
            vmem((rows, 2 * width), F32),
            vmem((n_exp * n_attn, CAP, HD), BF16),
            vmem((n_attn * n_exp, CAP, HD), BF16),
            sem((9,)),
            sem((groups,)),
            sem((groups,)),
            sem((n_z,)),
            sem((2,)),
            sem((2,)),
            sem,
            sem,
            sem((2, 2, 2, max(n_x, n_z) - 1)),
            sem((2, 2, max(n_x, n_z) - 1, max(n_x, n_z) - 1)),
            sem((2, 2, n_z, n_x)),
            sem((n_attn * CORES,)),
            sem((n_attn * CORES,)),
            sem,
            sem((n_z,)),
            sem,
            sem((n_attn,)),
        ],
        compiler_params=pltpu.CompilerParams(
            collective_id=0, has_side_effects=True, vmem_limit_bytes=58 * 1024 * 1024
        ),
        name="layer",
    )(
        lengths,
        residual,
        queries,
        keys,
        values,
        out_weight.reshape(heads // 2, 2, HD, HD),
        norm_gain.reshape(1, HD),
        expert_ids.T,
        gates.T,
        gate_up,
        down,
    )


def solution(mesh):
    in_specs = (
        P("attn", "expert"),
        P("expert", "attn"),
        P("expert", None, "attn"),
        P("expert", None, "attn"),
        P("expert"),
        P("attn", "expert"),
        P("expert"),
        P("attn", None),
        P("attn", None),
        P(("attn", "expert"), None, None),
        P(("attn", "expert"), None, None),
    )
    run = functools.partial(body, mesh.shape["attn"], mesh.shape["expert"])
    return jax.shard_map(
        run, mesh=mesh, in_specs=in_specs, out_specs=P("attn", "expert"), check_vma=False
    )
```
